512 devices in a mesh: state: 32 (over x, z), obs: 16 (over y, core).
Axes of the slice: x: 4, y: 8, z: 8, core: 2. Of those that a mesh axis runs over, the one named last changes fastest.
Arguments:
- state_mean: float32 [1024, 1024], P(('state', 'obs')), may hold values from -6 to 6
- state_anom: bfloat16 [1024, 80, 1024], P(('state', 'obs')), may hold values from -6 to 6
- obs_prior: bfloat16 [2, 80, 16384], P(None, None, ('state', 'obs')), may hold values from -6 to 6
- obs_value: bfloat16 [2, 16384], P(None, ('state', 'obs')), may hold values from -8 to 8
- obs_var: bfloat16 [2, 16384], P(None, ('state', 'obs')), may hold values from 0.29882812 to 3
- obs_weight: float32 [8, 16384], P(None, 'state'), may hold values from 0.1 to 0.5
- obs_home: int32 [16384], P('state'), may hold values from 0 to 131071, as said below
- tile_obs: int32 [2, 1024, 256], P(None, ('state', 'obs')), may hold values from 0 to 16383, as said below
- taper: bfloat16 [2, 1024, 256, 128], P(None, ('state', 'obs')), may hold values from 0.19921875 to 1
Outputs:
- analysis_mean: float32 [1024, 1024], P(('state', 'obs'))
- analysis_anom: bfloat16 [1024, 80, 1024], P(('state', 'obs'))
The draws below stay inside these ranges and needn't reach their ends.
Inputs may be any that keep to these rules, and one draw needn't show every extreme that they name: `tile_obs`: each tile's 256 entries of one colour are distinct observations, all owned by devices whose index along state differs from the tile's by at most one; observation numbers run owner by owner, 512 for each index of state. `obs_home`: each observation's column lies in a tile held by some device with the same index along state as the observation's owner.
All inputs are finite; a program needn't handle non-finite values.
Results may differ from the reference program's by a relative error of at most 0.009.
Values may be sent and summed in bfloat16 or wider, within the bound.
No kernel may reach another device: no remote copies, remote signals or barrier semaphores. Data moves between devices by JAX's collectives and lax.ppermute only.
A program may use at most 64 MiB of HBM per device.

```python
import math
import jax
import jax.numpy as jnp
from jax import lax

M = 80
LEV = 8
TILE = 128
JCAP = 256
COLORS = 2
TILE_DEV = 2
CELLS = 1024
NTILE = 1024
NOBS = 16384
NREGION = 512
REGION_TILES = 32


def draw_tile_obs(key, part):
    key = jax.random.fold_in(key, 11)
    tile_index = jnp.arange(NTILE, dtype=jnp.int32)
    region_of = tile_index // REGION_TILES
    region_total = NTILE // REGION_TILES
    candidate = jnp.arange(3 * NREGION, dtype=jnp.int32)
    cand_region = region_of[:, None] - 1 + candidate[None, :] // NREGION
    allowed = (cand_region >= 0) & (cand_region < region_total)
    scores = jax.random.randint(key, (COLORS, NTILE, 3 * NREGION), 0, 2 ** 18, dtype=jnp.int32)
    scores = scores * 8192 + candidate[None, None, :]
    scores = jnp.where(allowed[None], scores, -1)
    chosen = lax.top_k(scores, JCAP)[0] % 8192
    picked_region = region_of[None, :, None] - 1 + chosen // NREGION
    return (picked_region * NREGION + chosen % NREGION).astype(jnp.int32)


def draw_obs_home(key, part):
    key = jax.random.fold_in(key, 23)
    obs_index = jnp.arange(NOBS, dtype=jnp.int32)
    region_of = obs_index // NREGION
    offset = jax.random.randint(key, (NOBS,), 0, REGION_TILES * TILE, dtype=jnp.int32)
    return (region_of * (REGION_TILES * TILE) + offset).astype(jnp.int32)


def shard_levels(rng, extent, cuts, least, high):
    loudness = 1.0
    for position, shards_of in cuts:
        heights = jax.random.uniform(jax.random.fold_in(jax.random.fold_in(rng, 6), position), (shards_of,), jnp.float32, least / len(cuts), high / len(cuts))
        loudness = loudness * jnp.repeat(jnp.exp(heights), extent[position] // shards_of).reshape((-1,) + (1,) * (len(extent) - 1 - position))
    return loudness


def scatter_about(stream_key, dims, width, reach, split=(), kind=jnp.bfloat16):
    result = width * jax.random.normal(stream_key, dims, jnp.float32)
    if split:
        result = result * shard_levels(stream_key, dims, split, -0.22, 0.18)
    return jnp.clip(result, -reach, reach).astype(kind)


def setup_inputs(seed: int = 0) -> dict:
    key_of = jax.random.split(jax.random.key(seed), 10)
    return {
        "state_mean": scatter_about(key_of[0], (NTILE, CELLS), 1.0, 6.0, ((0, 512),), jnp.float32),
        "state_anom": scatter_about(key_of[1], (NTILE, M, CELLS), 1.0, 6.0, ((0, 512),)),
        "obs_prior": scatter_about(key_of[2], (COLORS, M, NOBS), 1.0, 6.0, ((2, 512),)),
        "obs_value": scatter_about(key_of[3], (COLORS, NOBS), 1.5, 8.0, ((1, 512),)),
        "obs_var": jnp.clip(jnp.exp(math.log(3.0) - 2.306499 * jax.random.uniform(key_of[4], (COLORS, NOBS), jnp.float32) ** shard_levels(key_of[4], (COLORS, NOBS), ((1, 512),), -0.2, 0.2)), 0.29882812, 3.0).astype(jnp.bfloat16),
        "obs_weight": jnp.clip(0.1 + 0.4 * jax.random.uniform(key_of[5], (LEV, NOBS), jnp.float32) ** shard_levels(key_of[5], (LEV, NOBS), ((1, 32),), -0.2, 0.2), 0.1, 0.5),
        "obs_home": draw_obs_home(jax.random.fold_in(key_of[9], 71), 0),
        "tile_obs": draw_tile_obs(jax.random.fold_in(key_of[9], 71), 0),
        "taper": jnp.clip(0.19921875 + 0.80078125 * jax.random.uniform(key_of[8], (COLORS, NTILE, JCAP, TILE), jnp.float32) ** shard_levels(key_of[8], (COLORS, NTILE, JCAP, TILE), ((1, 512),), -0.2, 0.2), 0.19921875, 1.0).astype(jnp.bfloat16),
    }


def obs_package(records):
    member_count = records.shape[0] - 2
    ensemble = records[:member_count].astype(jnp.float32)
    observed = records[member_count].astype(jnp.float32)
    error_var = records[member_count + 1].astype(jnp.float32)
    centre = lax.optimization_barrier(jnp.mean(ensemble, axis=0))
    anomaly = ensemble - centre
    spread = lax.optimization_barrier(jnp.sum(anomaly * anomaly, axis=0)) / (member_count - 1)
    kalman_gain = 1.0 / (spread + error_var)
    sqrt_factor = 1.0 / (1.0 + jnp.sqrt(error_var * kalman_gain))
    coef_anom = sqrt_factor * kalman_gain / (member_count - 1)
    coef_mean = kalman_gain * (observed - centre) / (member_count - 1)
    return (anomaly, coef_anom, coef_mean)

def reference(state_mean, state_anom, obs_prior, obs_value, obs_var, obs_weight, obs_home, tile_obs, taper):
    current_mean = state_mean
    current_anom = state_anom
    ensemble_now = obs_prior[0]
    group_count = NTILE // TILE_DEV
    for colour in range(COLORS):
        records = jnp.concatenate([ensemble_now, obs_value[colour][None], obs_var[colour][None]], 0)
        anomaly, coef_anom, coef_mean = obs_package(records)
        anomaly_rows = anomaly.T

        def one_group(pieces):
            group_mean, group_anom, obs_ids, group_taper = pieces
            basis_rows = anomaly_rows[obs_ids].astype(jnp.bfloat16).astype(jnp.float32)
            projection = jnp.einsum('tjm,tmc->tjc', basis_rows, group_anom.astype(jnp.float32), precision=lax.Precision.HIGHEST)
            proj_levels = projection.reshape(TILE_DEV, JCAP, LEV, TILE)
            taper_levels = group_taper.astype(jnp.float32)[:, :, None, :]
            mean_coef = coef_mean[obs_ids].reshape(TILE_DEV, JCAP, 1, 1)
            anom_coef = coef_anom[obs_ids].reshape(TILE_DEV, JCAP, 1, 1)
            new_mean = group_mean + lax.optimization_barrier(jnp.sum(taper_levels * mean_coef * proj_levels, axis=1)).reshape(TILE_DEV, CELLS)
            scaled = (taper_levels * anom_coef * proj_levels).astype(jnp.bfloat16).reshape(TILE_DEV, JCAP, CELLS)
            shift_term = jnp.einsum('tjm,tjc->tmc', basis_rows, scaled.astype(jnp.float32), precision=lax.Precision.HIGHEST)
            new_anom = (group_anom.astype(jnp.float32) - shift_term).astype(jnp.bfloat16)
            return (new_mean, new_anom)
        new_mean, new_anom = lax.map(one_group, (current_mean.reshape(group_count, TILE_DEV, CELLS), current_anom.reshape(group_count, TILE_DEV, M, CELLS), tile_obs[colour].reshape(group_count, TILE_DEV, JCAP), taper[colour].reshape(group_count, TILE_DEV, JCAP, TILE)))
        new_mean = new_mean.reshape(NTILE, CELLS)
        new_anom = new_anom.reshape(NTILE, M, CELLS)
        if colour == 0:
            home_tile = (obs_home // TILE).astype(jnp.int32)
            home_col = (obs_home % TILE).astype(jnp.int32)
            mean_change = (new_mean - current_mean).reshape(NTILE, LEV, TILE)[home_tile, :, home_col]
            before = current_anom.reshape(NTILE, M, LEV, TILE)[home_tile, :, :, home_col].astype(jnp.float32)
            updated = new_anom.reshape(NTILE, M, LEV, TILE)[home_tile, :, :, home_col].astype(jnp.float32)
            change = updated - before + mean_change[:, None, :]
            increment = jnp.einsum('jml,lj->mj', change, obs_weight, precision=lax.Precision.HIGHEST)
            ensemble_now = (obs_prior[1].astype(jnp.float32) + increment).astype(jnp.bfloat16)
        current_mean = new_mean
        current_anom = new_anom
    return (current_mean, current_anom)
```

```python
import functools

import jax
import jax.numpy as jnp
from jax import lax
from jax.experimental import pallas as pl
from jax.experimental.pallas import tpu as pltpu
from jax.sharding import Mesh
from jax.sharding import PartitionSpec as P

F32 = jnp.float32
BF16 = jnp.bfloat16
LANES = 128
VMEM = pl.BlockSpec(memory_space=pltpu.VMEM)
SMEM = pl.BlockSpec(memory_space=pltpu.SMEM)
PARAMS = pltpu.CompilerParams(vmem_limit_bytes=24 * 1024 * 1024)


def dot(a, b, contract=((1,), (0,))):
    return lax.dot_general(a, b, (contract, ((), ())), preferred_element_type=F32)


def iota(shape, dim):
    return lax.broadcasted_iota(jnp.int32, shape, dim)


def one_hot(mask):
    return jnp.where(mask, 1.0, 0.0).astype(BF16)


def identity(size):
    return one_hot(iota((size, size), 0) == iota((size, size), 1))


def pack_kernel(prior_ref, value_ref, var_ref, first_ref, second_ref):
    _, members, width = prior_ref.shape
    row = iota((16, width), 0)
    value = value_ref[...].astype(F32)
    var = var_ref[...].astype(F32)
    tail = jnp.where(row == 0, value[0:1], 0.0)
    tail = jnp.where(row == 1, var[0:1], tail)
    tail = jnp.where(row == 2, value[1:2], tail)
    tail = jnp.where(row == 3, var[1:2], tail).astype(BF16)
    rest = jnp.zeros((LANES - members - 16, width), BF16)
    blank = jnp.zeros((16, width), BF16)
    turn = identity(width)
    first = jnp.concatenate([prior_ref[0], tail, rest], axis=0)
    second = jnp.concatenate([prior_ref[1], blank, rest], axis=0)
    first_ref[...] = dot(turn, first, ((1,), (1,))).astype(BF16)
    second_ref[...] = dot(turn, second, ((1,), (1,))).astype(BF16)


def pick(fields, ids):
    slots = fields.shape[1]
    step = 512
    total = None
    for start in range(0, slots, step):
        chosen = one_hot(iota((step, ids.shape[1]), 0) + start == ids)
        part = dot(fields[:, start : start + step], chosen)
        total = part if total is None else total + part
    return total


def package(ensemble, value, var):
    members = ensemble.shape[0]
    centre = jnp.sum(ensemble, axis=0, keepdims=True) / members
    anomaly = ensemble - centre
    spread = jnp.sum(anomaly * anomaly, axis=0, keepdims=True) / (members - 1)
    gain = 1.0 / (spread + var)
    factor = 1.0 / (1.0 + jnp.sqrt(var * gain))
    coef_anom = factor * gain / (members - 1)
    coef_mean = gain * (value - centre) / (members - 1)
    return anomaly, coef_anom, coef_mean


def update_tile(picked, members, value_row, mean_ref, anom_ref, taper_ref, colour, tile, new_mean_ref, new_anom_ref, change_ref):
    value = picked[value_row : value_row + 1]
    var = picked[value_row + 1 : value_row + 2]
    anomaly, coef_anom, coef_mean = package(picked[:members], value, var)
    basis = anomaly.astype(BF16)
    listed = basis.shape[1]
    coefs = jnp.concatenate([coef_anom, coef_mean, jnp.zeros((6, listed), F32)], axis=0).T
    taper = taper_ref[colour, tile].astype(F32)
    taper_anom = taper * coefs[:, 0:1]
    taper_mean = taper * coefs[:, 1:2]
    width = taper.shape[1]
    step = 2 * width
    for start in range(0, anom_ref.shape[2], step):
        cells = slice(start, start + step)
        anom = anom_ref[tile, :, cells]
        projection = dot(basis, anom, ((0,), (0,)))
        low, high = projection[:, :width], projection[:, width:]
        scaled = jnp.concatenate([(taper_anom * low).astype(BF16), (taper_anom * high).astype(BF16)], axis=1)
        shift_mean = jnp.concatenate(
            [jnp.sum(taper_mean * low, axis=0, keepdims=True), jnp.sum(taper_mean * high, axis=0, keepdims=True)], axis=1
        )
        mean = mean_ref[tile : tile + 1, cells]
        new_mean = mean + shift_mean
        new_mean_ref[tile : tile + 1, cells] = new_mean
        old = anom.astype(F32)
        new_anom = (old - dot(basis, scaled)).astype(BF16)
        new_anom_ref[tile, :, cells] = new_anom
        if change_ref is not None:
            change = (new_anom.astype(F32) - old + (new_mean - mean)).astype(BF16)
            for part in range(2):
                change_ref[start // width + part, :, tile * width : (tile + 1) * width] = change[
                    :, part * width : (part + 1) * width
                ]


def first_kernel(
    place_ref, records_ref, lists_ref, home_ref, weight_ref, mean_ref, anom_ref, taper_ref,
    new_mean_ref, new_anom_ref, prior_ref, errors_ref, rows_ref, change_ref,
):
    tiles, members, _ = anom_ref.shape
    chips = records_ref.shape[1]
    width = records_ref.shape[2] // 4
    region = 2 * chips * width
    for chip in range(chips):
        at = chip * 2 * width
        rows_ref[at : at + 2 * width] = records_ref[0, chip, : 2 * width]
        rows_ref[2 * region + at : 2 * region + at + 2 * width] = records_ref[1, chip, : 2 * width]
        for core in range(2):
            here = at + core * width
            rows_ref[region + here : region + here + width] = records_ref[core, chip, 2 * width : 3 * width]
            rows_ref[3 * region + here : 3 * region + here + width] = records_ref[core, chip, 3 * width :]
    turn = identity(LANES)
    fields = dot(turn, rows_ref[...], ((1,), (1,)))
    listed = fields[: members + 16, : 3 * region].astype(BF16)
    errors_ref[...] = listed[members:]
    base = place_ref[0] * region
    for tile in range(tiles):
        picked = pick(listed, lists_ref[0, tile : tile + 1] - base)
        update_tile(
            picked, members, members, mean_ref, anom_ref, taper_ref, 0, tile, new_mean_ref, new_anom_ref, change_ref
        )
    home = home_ref[...] - place_ref[1]
    columns = change_ref.shape[2]
    at_home = one_hot(iota((columns, region), 0) == home)
    prior = fields[:members, 3 * region :]
    increment = None
    for level in range(change_ref.shape[0]):
        part = dot(change_ref[level], at_home) * weight_ref[level : level + 1]
        increment = part if increment is None else increment + part
    inside = (home >= 0) & (home < columns)
    updated = jnp.where(inside, prior + increment, 0.0).astype(BF16)
    half = region // 2
    prior_ref[0] = updated[:, :half]
    prior_ref[1] = updated[:, half:]


def second_kernel(
    place_ref, own_ref, beside_ref, errors_ref, lists_ref, mean_ref, anom_ref, taper_ref, new_mean_ref, new_anom_ref
):
    tiles, members, _ = anom_ref.shape
    ensemble = jnp.concatenate(
        [beside_ref[0, 0], beside_ref[0, 1], own_ref[0], own_ref[1], beside_ref[1, 0], beside_ref[1, 1]], axis=1
    )
    listed = jnp.concatenate([ensemble, errors_ref[...]], axis=0)
    region = own_ref.shape[0] * own_ref.shape[2]
    base = place_ref[0] * region
    for tile in range(tiles):
        picked = pick(listed, lists_ref[1, tile : tile + 1] - base)
        update_tile(
            picked, members, members + 2, mean_ref, anom_ref, taper_ref, 1, tile, new_mean_ref, new_anom_ref, None
        )


def beside(rows, chips, states):
    pairs = []
    for state in range(states):
        for chip in range(chips):
            if state + 1 < states:
                pairs.append(((state * chips + chip) * 2, ((state + 1) * chips + chip) * 2))
            if state > 0:
                pairs.append(((state * chips + chip) * 2 + 1, ((state - 1) * chips + chip) * 2 + 1))
    return lax.ppermute(rows, ("state", "chip", "core"), pairs)


def local(state_mean, state_anom, obs_prior, obs_value, obs_var, obs_weight, obs_home, tile_obs, taper):
    tiles, members, cells = state_anom.shape
    tile_width = taper.shape[3]
    chips, states = lax.axis_size("chip"), lax.axis_size("state")
    width = obs_prior.shape[2]
    region = 2 * chips * width
    state, chip, core = lax.axis_index("state"), lax.axis_index("chip"), lax.axis_index("core")
    first_column = ((state * chips + chip) * 2 + core) * tiles * tile_width
    place = jnp.stack([state - 1, first_column]).astype(jnp.int32)

    block = jax.ShapeDtypeStruct((width, LANES), BF16)
    first, second = pl.pallas_call(
        pack_kernel, out_shape=(block, block), in_specs=[VMEM] * 3, out_specs=(VMEM, VMEM), name="pack"
    )(obs_prior, obs_value, obs_var)
    pair = lax.all_gather(first, "core", axis=0, tiled=True)
    near = beside(pair, chips, states)
    sent = jnp.concatenate([near, first, second], axis=0)
    sent = jnp.broadcast_to(sent[None], (chips, 4 * width, LANES))
    got = lax.all_to_all(sent, "chip", 0, 0)
    records = lax.all_gather(got, "core", axis=0)

    state_shapes = (
        jax.ShapeDtypeStruct(state_mean.shape, state_mean.dtype),
        jax.ShapeDtypeStruct(state_anom.shape, state_anom.dtype),
    )
    new_mean, new_anom, priors, errors = pl.pallas_call(
        first_kernel,
        out_shape=state_shapes
        + (
            jax.ShapeDtypeStruct((2, members, region // 2), BF16),
            jax.ShapeDtypeStruct((16, 3 * region), BF16),
        ),
        in_specs=[SMEM] + [VMEM] * 7,
        out_specs=(VMEM,) * 4,
        scratch_shapes=[
            pltpu.VMEM((4 * region, LANES), BF16),
            pltpu.VMEM((cells // tile_width, members, tiles * tile_width), BF16),
        ],
        compiler_params=PARAMS,
        name="first",
    )(place, records, tile_obs, obs_home[None], obs_weight, state_mean, state_anom, taper)

    shared = lax.all_gather(priors, "core", axis=0)
    half = lax.dynamic_index_in_dim(shared, core, axis=1, keepdims=False)
    half = half[0] + half[1]
    halves = lax.all_to_all(jnp.broadcast_to(half[None], (chips,) + half.shape), "chip", 0, 0)
    total = jnp.sum(halves, axis=0, dtype=BF16)
    own = lax.all_gather(total, "core", axis=0)
    sides = lax.all_gather(beside(own, chips, states), "core", axis=0)

    return pl.pallas_call(
        second_kernel,
        out_shape=state_shapes,
        in_specs=[SMEM] + [VMEM] * 7,
        out_specs=(VMEM,) * 2,
        compiler_params=PARAMS,
        name="second",
    )(place, own, sides, errors, tile_obs, new_mean, new_anom, taper)


def solution(mesh):
    states, columns = mesh.shape["state"], mesh.shape["obs"]
    fine = Mesh(mesh.devices.reshape(states, columns // 2, 2), ("state", "chip", "core"))
    every = ("state", "chip", "core")
    in_specs = (
        P(every, None),
        P(every, None, None),
        P(None, None, every),
        P(None, every),
        P(None, every),
        P(None, "state"),
        P("state"),
        P(None, every, None),
        P(None, every, None, None),
    )
    out_specs = (P(every, None), P(every, None, None))
    return jax.shard_map(local, mesh=fine, in_specs=in_specs, out_specs=out_specs, check_vma=False)
```

```python
import functools

import jax
import jax.numpy as jnp
from jax import lax
from jax.experimental import pallas as pl
from jax.experimental.pallas import tpu as pltpu
from jax.sharding import Mesh
from jax.sharding import PartitionSpec as P

F32 = jnp.float32
BF16 = jnp.bfloat16
LANES = 128
SLOTS = 128
VMEM = pl.BlockSpec(memory_space=pltpu.VMEM)
SMEM = pl.BlockSpec(memory_space=pltpu.SMEM)
PARAMS = pltpu.CompilerParams(vmem_limit_bytes=24 * 1024 * 1024)


def dot(a, b, contract=((1,), (0,))):
    return lax.dot_general(a, b, (contract, ((), ())), preferred_element_type=F32)


def iota(shape, dim):
    return lax.broadcasted_iota(jnp.int32, shape, dim)


def one_hot(mask):
    return jnp.where(mask, 1.0, 0.0).astype(BF16)


def identity(size):
    return one_hot(iota((size, size), 0) == iota((size, size), 1))


def pack_kernel(prior_ref, value_ref, var_ref, rows_ref):
    _, width, members = prior_ref.shape
    row = iota((LANES, width), 0) - members
    value = value_ref[...].astype(F32)
    var = var_ref[...].astype(F32)
    tail = jnp.where(row == 0, value[0:1], 0.0)
    tail = jnp.where(row == 1, var[0:1], tail)
    tail = jnp.where(row == 2, value[1:2], tail)
    tail = jnp.where(row == 3, var[1:2], tail).astype(BF16)
    spread = one_hot(iota((members, LANES), 0) == iota((members, LANES), 1))
    first = dot(prior_ref[0], spread) + dot(identity(width), tail, ((1,), (1,)))
    second = dot(prior_ref[1], spread)
    for copy in range(rows_ref.shape[0]):
        rows_ref[copy, 0] = first.astype(BF16)
        rows_ref[copy, 1] = second.astype(BF16)


def pick(fields, ids):
    slots = fields.shape[1]
    step = 512
    total = None
    for start in range(0, slots, step):
        chosen = one_hot(iota((step, ids.shape[1]), 0) + start == ids)
        part = dot(fields[:, start : start + step], chosen)
        total = part if total is None else total + part
    return total


def package(ensemble, value, var):
    members = ensemble.shape[0]
    centre = jnp.sum(ensemble, axis=0, keepdims=True) / members
    anomaly = ensemble - centre
    spread = jnp.sum(anomaly * anomaly, axis=0, keepdims=True) / (members - 1)
    gain = 1.0 / (spread + var)
    factor = 1.0 / (1.0 + jnp.sqrt(var * gain))
    coef_anom = factor * gain / (members - 1)
    coef_mean = gain * (value - centre) / (members - 1)
    return anomaly, coef_anom, coef_mean


def scale_tile(picked, members, value_row, mean_ref, anom_ref, taper_ref, colour, tile, new_mean_ref, scaled_ref):
    value = picked[value_row : value_row + 1]
    var = picked[value_row + 1 : value_row + 2]
    anomaly, coef_anom, coef_mean = package(picked[:members], value, var)
    basis = anomaly.astype(BF16)
    listed = basis.shape[1]
    coefs = jnp.concatenate([coef_anom, coef_mean, jnp.zeros((6, listed), F32)], axis=0).T
    taper = taper_ref[colour, tile].astype(F32)
    taper_anom = taper * coefs[:, 0:1]
    taper_mean = taper * coefs[:, 1:2]
    width = taper.shape[1]
    step = 2 * width
    for start in range(0, anom_ref.shape[2], step):
        projection = dot(basis, anom_ref[tile, :, start : start + step], ((0,), (0,)))
        for part in range(0, step, width):
            cells = slice(start + part, start + part + width)
            level = projection[:, part : part + width]
            scaled_ref[tile, :, cells] = (taper_anom * level).astype(BF16)
            shift = jnp.sum(taper_mean * level, axis=0, keepdims=True)
            new_mean_ref[tile : tile + 1, cells] = mean_ref[tile : tile + 1, cells] + shift
    return basis


def shift_tile(basis, mean_ref, anom_ref, tile, new_mean_ref, new_anom_ref, scaled_ref, width, change_ref):
    step = 2 * width
    for start in range(0, anom_ref.shape[2], step):
        cells = slice(start, start + step)
        old = anom_ref[tile, :, cells].astype(F32)
        new_anom = (old - dot(basis, scaled_ref[tile, :, cells])).astype(BF16)
        new_anom_ref[tile, :, cells] = new_anom
        if change_ref is not None:
            rise = new_mean_ref[tile : tile + 1, cells] - mean_ref[tile : tile + 1, cells]
            change = (new_anom.astype(F32) - old + rise).astype(BF16)
            for part in range(2):
                change_ref[start // width + part, :, tile * width : (tile + 1) * width] = change[
                    :, part * width : (part + 1) * width
                ]


def update_tiles(
    listed, lists_ref, colour, base, members, value_row, mean_ref, anom_ref, taper_ref,
    new_mean_ref, new_anom_ref, scaled_ref, change_ref,
):
    bases = []
    for tile in range(anom_ref.shape[0]):
        picked = pick(listed, lists_ref[colour, tile : tile + 1] - base)
        bases.append(
            scale_tile(
                picked, members, value_row, mean_ref, anom_ref, taper_ref, colour, tile, new_mean_ref, scaled_ref
            )
        )
    for tile, basis in enumerate(bases):
        shift_tile(
            basis, mean_ref, anom_ref, tile, new_mean_ref, new_anom_ref, scaled_ref, taper_ref.shape[3], change_ref
        )


def plan_kernel(chips, chip_columns, place_ref, home_ref, slot_ref, near_ref, crowded_ref):
    region = home_ref.shape[1]
    column = home_ref[...] - place_ref[2]
    near_ref[...] = home_ref[...] - place_ref[1]
    chip = jnp.zeros_like(column)
    for edge in range(1, chips):
        chip = chip + jnp.where(column >= edge * chip_columns, 1, 0)
    chip = chip.astype(F32)
    across = jnp.broadcast_to(chip, (8, region)).T[:, 0:1]
    earlier = (across == chip) & (iota((region, region), 0) < iota((region, region), 1))
    rank = jnp.sum(jnp.where(earlier, 1.0, 0.0), axis=0, keepdims=True)
    slot_ref[...] = (chip * SLOTS + rank).astype(jnp.int32)
    crowded_ref[0] = (jnp.max(rank) >= SLOTS).astype(jnp.int32)


def first_kernel(
    place_ref, row_ref, beside_ref, lists_ref, home_ref, slot_ref, weight_ref, mean_ref, anom_ref, taper_ref,
    new_mean_ref, new_anom_ref, packed_ref, prior_ref, errors_ref, rows_ref, scaled_ref, change_ref,
):
    members = anom_ref.shape[1]
    _, chips, _, width, _ = row_ref.shape
    region = 2 * chips * width
    for chip in range(chips):
        for core in range(2):
            at = (chip * 2 + core) * width
            for part, block in enumerate(
                (beside_ref[0, 0, core, chip], row_ref[core, chip, 0], beside_ref[1, 1, core, chip], row_ref[core, chip, 1])
            ):
                rows_ref[part * region + at : part * region + at + width] = block
    turn = identity(LANES)
    fields = dot(turn, rows_ref[...], ((1,), (1,)))
    listed = fields[: members + 16, : 3 * region].astype(BF16)
    errors_ref[...] = listed[members:]
    base = place_ref[0] * region
    update_tiles(
        listed, lists_ref, 0, base, members, members, mean_ref, anom_ref, taper_ref,
        new_mean_ref, new_anom_ref, scaled_ref, change_ref,
    )
    home = home_ref[...]
    columns = change_ref.shape[2]
    at_home = one_hot(iota((columns, region), 0) == home)
    prior = fields[:members, 3 * region :]
    increment = None
    for level in range(change_ref.shape[0]):
        part = dot(change_ref[level], at_home) * weight_ref[level : level + 1]
        increment = part if increment is None else increment + part
    inside = (home >= 0) & (home < columns)
    updated = jnp.where(inside, prior + increment, 0.0).astype(BF16)
    prior_ref[...] = updated
    to_slot = one_hot(iota((SLOTS, region), 0) + place_ref[3] * SLOTS == slot_ref[...])
    packed_ref[...] = dot(updated, to_slot, ((1,), (1,))).astype(BF16)


def spread_kernel(packed_ref, slot_ref, prior_ref):
    region = slot_ref.shape[1]
    total = None
    for chip in range(packed_ref.shape[0]):
        from_slot = one_hot(iota((SLOTS, region), 0) + chip * SLOTS == slot_ref[...])
        part = dot(packed_ref[chip], from_slot)
        total = part if total is None else total + part
    prior_ref[...] = total.astype(BF16)


def second_kernel(
    place_ref, own_ref, beside_ref, errors_ref, lists_ref, mean_ref, anom_ref, taper_ref,
    new_mean_ref, new_anom_ref, scaled_ref,
):
    members = anom_ref.shape[1]
    ensemble = jnp.concatenate([beside_ref[0, 0], own_ref[...], beside_ref[1, 1]], axis=1)
    listed = jnp.concatenate([ensemble, errors_ref[...]], axis=0)
    base = place_ref[0] * own_ref.shape[1]
    update_tiles(
        listed, lists_ref, 1, base, members, members + 2, mean_ref, anom_ref, taper_ref,
        new_mean_ref, new_anom_ref, scaled_ref, None,
    )


def beside(rows, chips, states):
    at = lambda state, chip, core: (state * chips + chip) * 2 + core
    groups = [[at(s, c, 1), at(s + 1, c, 0)] for s in range(states - 1) for c in range(chips)]
    for state, core in ((0, 0), (states - 1, 1)):
        groups += [[at(state, c, core), at(state, c + 1, core)] for c in range(0, chips, 2)]
    swapped = lax.all_gather(rows, ("state", "chip", "core"), axis_index_groups=groups)
    return lax.all_gather(swapped, "core")


def local(state_mean, state_anom, obs_prior, obs_value, obs_var, obs_weight, obs_home, tile_obs, taper):
    tiles, members, cells = state_anom.shape
    tile_width = taper.shape[3]
    chips, states = lax.axis_size("chip"), lax.axis_size("state")
    width = obs_prior.shape[2]
    region = 2 * chips * width
    state, chip, core = lax.axis_index("state"), lax.axis_index("chip"), lax.axis_index("core")
    chip_columns = 2 * tiles * tile_width
    row_column = state * chips * chip_columns
    first_column = row_column + chip * chip_columns + core * tiles * tile_width
    place = jnp.stack([state - 1, first_column, row_column, chip]).astype(jnp.int32)

    sent = pl.pallas_call(
        pack_kernel,
        out_shape=jax.ShapeDtypeStruct((chips, 2, width, LANES), BF16),
        in_specs=[VMEM] * 3,
        out_specs=VMEM,
        name="pack",
    )(jnp.swapaxes(obs_prior, 1, 2), obs_value, obs_var)
    row = lax.all_gather(lax.all_to_all(sent, "chip", 0, 0), "core", axis=0)
    near = beside(row[:, :, 0], chips, states)

    slot, home, crowded = pl.pallas_call(
        functools.partial(plan_kernel, chips, chip_columns),
        out_shape=(jax.ShapeDtypeStruct((1, region), jnp.int32),) * 2 + (jax.ShapeDtypeStruct((1,), jnp.int32),),
        in_specs=[SMEM, VMEM],
        out_specs=(VMEM, VMEM, SMEM),
        name="plan",
    )(place, obs_home[None])

    state_shapes = (
        jax.ShapeDtypeStruct(state_mean.shape, state_mean.dtype),
        jax.ShapeDtypeStruct(state_anom.shape, state_anom.dtype),
    )
    scaled = pltpu.VMEM((tiles, tile_obs.shape[2], cells), BF16)
    prior_shape = jax.ShapeDtypeStruct((members, region), BF16)
    new_mean, new_anom, packed, prior, errors = pl.pallas_call(
        first_kernel,
        out_shape=state_shapes
        + (
            jax.ShapeDtypeStruct((members, SLOTS), BF16),
            prior_shape,
            jax.ShapeDtypeStruct((16, 3 * region), BF16),
        ),
        in_specs=[SMEM] + [VMEM] * 9,
        out_specs=(VMEM,) * 5,
        scratch_shapes=[
            pltpu.VMEM((4 * region, LANES), BF16),
            scaled,
            pltpu.VMEM((cells // tile_width, members, tiles * tile_width), BF16),
        ],
        compiler_params=PARAMS,
        name="first",
    )(place, row, near, tile_obs, home, slot, obs_weight, state_mean, state_anom, taper)

    def to_row(part):
        both = lax.all_gather(part, "core", axis=0)
        both = both[0] + both[1]
        return lax.all_to_all(jnp.broadcast_to(both[None], (chips,) + both.shape), "chip", 0, 0)

    def by_slot(packed, prior, slot):
        return pl.pallas_call(
            spread_kernel, out_shape=prior_shape, in_specs=[VMEM] * 2, out_specs=VMEM, name="spread"
        )(to_row(packed), slot)

    def whole(packed, prior, slot):
        return jnp.sum(to_row(prior), axis=0, dtype=BF16)

    own = lax.cond(crowded[0] == 0, by_slot, whole, packed, prior, slot)
    sides = beside(own, chips, states)

    return pl.pallas_call(
        second_kernel,
        out_shape=state_shapes,
        in_specs=[SMEM] + [VMEM] * 7,
        out_specs=(VMEM,) * 2,
        scratch_shapes=[scaled],
        compiler_params=PARAMS,
        name="second",
    )(place, own, sides, errors, tile_obs, new_mean, new_anom, taper)


def solution(mesh):
    states, columns = mesh.shape["state"], mesh.shape["obs"]
    fine = Mesh(mesh.devices.reshape(states, columns // 2, 2), ("state", "chip", "core"))
    every = ("state", "chip", "core")
    in_specs = (
        P(every, None),
        P(every, None, None),
        P(None, None, every),
        P(None, every),
        P(None, every),
        P(None, "state"),
        P("state"),
        P(None, every, None),
        P(None, every, None, None),
    )
    out_specs = (P(every, None), P(every, None, None))
    return jax.shard_map(local, mesh=fine, in_specs=in_specs, out_specs=out_specs, check_vma=False)
```

```python
import functools

import jax
import jax.numpy as jnp
from jax import lax
from jax.experimental import pallas as pl
from jax.experimental.pallas import tpu as pltpu
from jax.sharding import Mesh
from jax.sharding import PartitionSpec as P

F32 = jnp.float32
BF16 = jnp.bfloat16
LANES = 128
SLOTS = 64
SLOT, MINE, NEAR, LISTS = 0, 1, 2, 3
VMEM = pl.BlockSpec(memory_space=pltpu.VMEM)
SMEM = pl.BlockSpec(memory_space=pltpu.SMEM)
SMALL = pltpu.CompilerParams(vmem_limit_bytes=8 * 1024 * 1024)
LARGE = pltpu.CompilerParams(vmem_limit_bytes=24 * 1024 * 1024)


def dot(a, b, contract=((1,), (0,))):
    return lax.dot_general(a, b, (contract, ((), ())), preferred_element_type=F32)


def iota(shape, dim):
    return lax.broadcasted_iota(jnp.int32, shape, dim)


def one_hot(mask):
    return jnp.where(mask, 1.0, 0.0).astype(BF16)


def identity(size):
    return one_hot(iota((size, size), 0) == iota((size, size), 1))


def pack_kernel(prior_in, value_in, var_in, rows_ref, prior_ref, value_ref, var_ref, sems):
    copies = [
        pltpu.make_async_copy(source, target, sems.at[i])
        for i, (source, target) in enumerate(((prior_in, prior_ref), (value_in, value_ref), (var_in, var_ref)))
    ]
    for copy in copies:
        copy.start()
    for copy in copies:
        copy.wait()
    _, width, members = prior_ref.shape
    row = iota((LANES, width), 0) - members
    value = value_ref[...].astype(F32)
    var = var_ref[...].astype(F32)
    tail = jnp.where(row == 0, value[0:1], 0.0)
    tail = jnp.where(row == 1, var[0:1], tail)
    tail = jnp.where(row == 2, value[1:2], tail)
    tail = jnp.where(row == 3, var[1:2], tail).astype(BF16)
    spread = one_hot(iota((members, LANES), 0) == iota((members, LANES), 1))
    first = dot(prior_ref[0], spread) + dot(identity(width), tail, ((1,), (1,)))
    second = dot(prior_ref[1], spread)
    for copy in range(rows_ref.shape[0]):
        rows_ref[copy, 0] = first.astype(BF16)
        rows_ref[copy, 1] = second.astype(BF16)


def pick(fields, ids):
    slots = fields.shape[1]
    step = 512
    total = None
    for start in range(0, slots, step):
        chosen = one_hot(iota((step, ids.shape[1]), 0) + start == ids)
        part = dot(fields[:, start : start + step], chosen)
        total = part if total is None else total + part
    return total


def package(ensemble, value, var):
    members = ensemble.shape[0]
    centre = jnp.sum(ensemble, axis=0, keepdims=True) / members
    anomaly = ensemble - centre
    spread = jnp.sum(anomaly * anomaly, axis=0, keepdims=True) / (members - 1)
    gain = 1.0 / (spread + var)
    factor = 1.0 / (1.0 + jnp.sqrt(var * gain))
    coef_anom = factor * gain / (members - 1)
    coef_mean = gain * (value - centre) / (members - 1)
    return anomaly, coef_anom, coef_mean


def scale_tile(picked, members, value_row, mean_ref, anom_ref, taper_ref, colour, tile, new_mean_ref, scaled_ref):
    value = picked[value_row : value_row + 1]
    var = picked[value_row + 1 : value_row + 2]
    anomaly, coef_anom, coef_mean = package(picked[:members], value, var)
    basis = anomaly.astype(BF16)
    listed = basis.shape[1]
    coefs = jnp.concatenate([coef_anom, coef_mean, jnp.zeros((6, listed), F32)], axis=0).T
    taper = taper_ref[colour, tile].astype(F32)
    taper_anom = taper * coefs[:, 0:1]
    taper_mean = taper * coefs[:, 1:2]
    width = taper.shape[1]
    step = 2 * width
    for start in range(0, anom_ref.shape[2], step):
        projection = dot(basis, anom_ref[tile, :, start : start + step], ((0,), (0,)))
        for part in range(0, step, width):
            cells = slice(start + part, start + part + width)
            level = projection[:, part : part + width]
            scaled_ref[tile, :, cells] = (taper_anom * level).astype(BF16)
            shift = jnp.sum(taper_mean * level, axis=0, keepdims=True)
            new_mean_ref[tile : tile + 1, cells] = mean_ref[tile : tile + 1, cells] + shift
    return basis


def shift_tile(basis, mean_ref, anom_ref, tile, new_mean_ref, new_anom_ref, scaled_ref, width, change_ref):
    step = 2 * width
    for start in range(0, anom_ref.shape[2], step):
        cells = slice(start, start + step)
        old = anom_ref[tile, :, cells].astype(F32)
        new_anom = (old - dot(basis, scaled_ref[tile, :, cells])).astype(BF16)
        new_anom_ref[tile, :, cells] = new_anom
        if change_ref is not None:
            rise = new_mean_ref[tile : tile + 1, cells] - mean_ref[tile : tile + 1, cells]
            change = (new_anom.astype(F32) - old + rise).astype(BF16)
            for part in range(2):
                change_ref[start // width + part, :, tile * width : (tile + 1) * width] = change[
                    :, part * width : (part + 1) * width
                ]


def update_tiles(
    listed, table_ref, colour, members, value_row, mean_ref, anom_ref, taper_ref,
    new_mean_ref, new_anom_ref, scaled_ref, change_ref,
):
    bases = []
    length = taper_ref.shape[2]
    for tile in range(anom_ref.shape[0]):
        ids = table_ref[LISTS + colour : LISTS + colour + 1, tile * length : (tile + 1) * length]
        picked = pick(listed, ids)
        bases.append(
            scale_tile(
                picked, members, value_row, mean_ref, anom_ref, taper_ref, colour, tile, new_mean_ref, scaled_ref
            )
        )
    for tile, basis in enumerate(bases):
        shift_tile(
            basis, mean_ref, anom_ref, tile, new_mean_ref, new_anom_ref, scaled_ref, taper_ref.shape[3], change_ref
        )


def plan_kernel(chips, tile_columns, home_ref, lists_ref, table_ref, crowded_ref):
    colours, tiles, length = lists_ref.shape
    region = home_ref.shape[1]
    state, own_chip, core = lax.axis_index("state"), lax.axis_index("chip"), lax.axis_index("core")
    device_columns = tiles * tile_columns
    own = own_chip * 2 + core
    column = home_ref[...] - state * (chips * 2 * device_columns)
    device = jnp.zeros_like(column)
    for edge in range(1, chips * 2):
        device = device + jnp.where(column >= edge * device_columns, 1, 0)
    device = device.astype(F32)
    across = jnp.broadcast_to(device, (8, region)).T[:, 0:1]
    earlier = (across == device) & (iota((region, region), 0) < iota((region, region), 1))
    rank = jnp.sum(jnp.where(earlier, 1.0, 0.0), axis=0, keepdims=True)
    slot = (device * SLOTS + rank).astype(jnp.int32)
    table_ref[SLOT : SLOT + 1] = slot
    table_ref[MINE : MINE + 1] = slot - own * SLOTS
    table_ref[NEAR : NEAR + 1] = column - own * device_columns
    for colour in range(colours):
        for tile in range(tiles):
            table_ref[LISTS + colour : LISTS + colour + 1, tile * length : (tile + 1) * length] = (
                lists_ref[colour, tile : tile + 1] - (state - 1) * region
            )
    crowded_ref[0] = (jnp.max(rank) >= SLOTS).astype(jnp.int32)


def first_kernel(
    row_ref, beside_ref, table_ref, weight_ref, mean_ref, anom_ref, taper_ref,
    new_mean_ref, new_anom_ref, packed_ref, prior_ref, errors_ref, rows_ref, scaled_ref, change_ref,
):
    members = anom_ref.shape[1]
    _, chips, _, width, _ = row_ref.shape
    region = 2 * chips * width
    for chip in range(chips):
        for core in range(2):
            at = (chip * 2 + core) * width
            for part, block in enumerate(
                (beside_ref[0, core, chip], row_ref[core, chip, 0], beside_ref[1, core, chip], row_ref[core, chip, 1])
            ):
                rows_ref[part * region + at : part * region + at + width] = block
    turn = identity(LANES)
    fields = dot(turn, rows_ref[...], ((1,), (1,)))
    listed = fields[: members + 16, : 3 * region].astype(BF16)
    errors_ref[...] = listed[members:]
    update_tiles(
        listed, table_ref, 0, members, members, mean_ref, anom_ref, taper_ref,
        new_mean_ref, new_anom_ref, scaled_ref, change_ref,
    )
    home = table_ref[NEAR : NEAR + 1]
    columns = change_ref.shape[2]
    at_home = one_hot(iota((columns, region), 0) == home)
    prior = fields[:members, 3 * region :]
    increment = None
    for level in range(change_ref.shape[0]):
        part = dot(change_ref[level], at_home) * weight_ref[level : level + 1]
        increment = part if increment is None else increment + part
    inside = (home >= 0) & (home < columns)
    updated = jnp.where(inside, prior + increment, 0.0).astype(BF16)
    prior_ref[...] = updated
    lane = iota((LANES, region), 0)
    to_slot = one_hot(jnp.where(lane < SLOTS, lane, lane - SLOTS) == table_ref[MINE : MINE + 1])
    twice = dot(updated, to_slot, ((1,), (1,)))
    half = members // 2
    packed_ref[...] = jnp.where(iota((half, LANES), 1) < SLOTS, twice[:half], twice[half:]).astype(BF16)


def spread_kernel(packed_ref, table_ref, prior_ref):
    region = table_ref.shape[1]
    _, chips, half, _ = packed_ref.shape
    first = iota((half, LANES), 1) < SLOTS
    rows = iota((2 * SLOTS, region), 0)
    total = None
    for chip in range(chips):
        low, high = packed_ref[0, chip].astype(F32), packed_ref[1, chip].astype(F32)
        upper = jnp.where(first, low, pltpu.roll(high, SLOTS, 1))
        lower = jnp.where(first, pltpu.roll(low, SLOTS, 1), high)
        ensemble = jnp.concatenate([upper, lower], axis=0).astype(BF16)
        part = dot(ensemble, one_hot(rows + chip * 2 * SLOTS == table_ref[SLOT : SLOT + 1]))
        total = part if total is None else total + part
    prior_ref[...] = total.astype(BF16)


def second_kernel(
    own_ref, beside_ref, errors_ref, table_ref, mean_ref, anom_ref, taper_ref,
    new_mean_ref, new_anom_ref, scaled_ref,
):
    members = anom_ref.shape[1]
    ensemble = jnp.concatenate([beside_ref[0], own_ref[...], beside_ref[1]], axis=1)
    listed = jnp.concatenate([ensemble, errors_ref[...]], axis=0)
    update_tiles(
        listed, table_ref, 1, members, members + 2, mean_ref, anom_ref, taper_ref,
        new_mean_ref, new_anom_ref, scaled_ref, None,
    )


def beside(rows, chips, states):
    at = lambda state, chip, core: (state * chips + chip) * 2 + core
    groups = [[at(s, c, 1), at(s + 1, c, 0)] for s in range(states - 1) for c in range(chips)]
    for state, core in ((0, 0), (states - 1, 1)):
        groups += [[at(state, c, core), at(state, c + 1, core)] for c in range(0, chips, 2)]
    swapped = lax.all_gather(rows, ("state", "chip", "core"), axis_index_groups=groups)
    partner = lax.dynamic_index_in_dim(swapped, lax.axis_index("core"), axis=0, keepdims=False)
    return lax.all_gather(partner, "core")


def local(state_mean, state_anom, obs_prior, obs_value, obs_var, obs_weight, obs_home, tile_obs, taper):
    tiles, members, cells = state_anom.shape
    tile_width = taper.shape[3]
    chips, states = lax.axis_size("chip"), lax.axis_size("state")
    width = obs_prior.shape[2]
    region = 2 * chips * width
    raw = (jnp.swapaxes(obs_prior, 1, 2), obs_value, obs_var)
    sent = pl.pallas_call(
        pack_kernel,
        out_shape=pltpu.VMEM((chips, 2, width, LANES), BF16),
        in_specs=[pl.BlockSpec(memory_space=pltpu.HBM)] * 3,
        out_specs=VMEM,
        scratch_shapes=[pltpu.VMEM(a.shape, a.dtype) for a in raw] + [pltpu.SemaphoreType.DMA((3,))],
        compiler_params=SMALL,
        name="pack",
    )(*[pltpu.with_memory_space_constraint(a, pltpu.HBM) for a in raw])
    row = lax.all_gather(lax.all_to_all(sent, "chip", 0, 0), "core", axis=0)
    near = beside(row[:, :, 0], chips, states)

    table, crowded = pl.pallas_call(
        functools.partial(plan_kernel, chips, tile_width),
        out_shape=(jax.ShapeDtypeStruct((8, region), jnp.int32), jax.ShapeDtypeStruct((1,), jnp.int32)),
        in_specs=[VMEM] * 2,
        out_specs=(VMEM, SMEM),
        compiler_params=SMALL,
        name="plan",
    )(obs_home[None], tile_obs)

    state_shapes = (
        jax.ShapeDtypeStruct(state_mean.shape, state_mean.dtype),
        jax.ShapeDtypeStruct(state_anom.shape, state_anom.dtype),
    )
    scaled = pltpu.VMEM((tiles, tile_obs.shape[2], cells), BF16)
    prior_shape = jax.ShapeDtypeStruct((members, region), BF16)
    new_mean, new_anom, packed, prior, errors = pl.pallas_call(
        first_kernel,
        out_shape=state_shapes
        + (
            jax.ShapeDtypeStruct((members // 2, LANES), BF16),
            prior_shape,
            jax.ShapeDtypeStruct((16, 3 * region), BF16),
        ),
        in_specs=[VMEM] * 7,
        out_specs=(VMEM,) * 5,
        scratch_shapes=[
            pltpu.VMEM((4 * region, LANES), BF16),
            scaled,
            pltpu.VMEM((cells // tile_width, members, tiles * tile_width), BF16),
        ],
        compiler_params=LARGE,
        name="first",
    )(row, near, table, obs_weight, state_mean, state_anom, taper)

    def to_row(part):
        return lax.all_to_all(jnp.broadcast_to(part[None], (chips,) + part.shape), "chip", 0, 0)

    def by_slot(packed, prior, table):
        return pl.pallas_call(
            spread_kernel,
            out_shape=prior_shape,
            in_specs=[VMEM] * 2,
            out_specs=VMEM,
            compiler_params=SMALL,
            name="spread",
        )(lax.all_gather(to_row(packed), "core"), table)

    def whole(packed, prior, table):
        both = lax.all_gather(prior, "core")
        return jnp.sum(to_row(both[0] + both[1]), axis=0, dtype=BF16)

    own = lax.cond(crowded[0] == 0, by_slot, whole, packed, prior, table)
    sides = beside(own, chips, states)

    return pl.pallas_call(
        second_kernel,
        out_shape=state_shapes,
        in_specs=[VMEM] * 7,
        out_specs=(VMEM,) * 2,
        scratch_shapes=[scaled],
        compiler_params=LARGE,
        name="second",
    )(own, sides, errors, table, new_mean, new_anom, taper)


def solution(mesh):
    states, columns = mesh.shape["state"], mesh.shape["obs"]
    fine = Mesh(mesh.devices.reshape(states, columns // 2, 2), ("state", "chip", "core"))
    every = ("state", "chip", "core")
    in_specs = (
        P(every, None),
        P(every, None, None),
        P(None, None, every),
        P(None, every),
        P(None, every),
        P(None, "state"),
        P("state"),
        P(None, every, None),
        P(None, every, None, None),
    )
    out_specs = (P(every, None), P(every, None, None))
    return jax.shard_map(local, mesh=fine, in_specs=in_specs, out_specs=out_specs, check_vma=False)
```

```python
import functools

import jax
import jax.numpy as jnp
from jax import lax
from jax.experimental import pallas as pl
from jax.experimental.pallas import tpu as pltpu
from jax.sharding import Mesh
from jax.sharding import PartitionSpec as P

F32 = jnp.float32
BF16 = jnp.bfloat16
LANES = 128
SLOTS = 64
SLOT, MINE, NEAR, LISTS = 0, 1, 2, 3
VMEM = pl.BlockSpec(memory_space=pltpu.VMEM)
SMEM = pl.BlockSpec(memory_space=pltpu.SMEM)
SMALL = pltpu.CompilerParams(vmem_limit_bytes=8 * 1024 * 1024)
LARGE = pltpu.CompilerParams(vmem_limit_bytes=24 * 1024 * 1024)


def dot(a, b, contract=((1,), (0,))):
    return lax.dot_general(a, b, (contract, ((), ())), preferred_element_type=F32)


def iota(shape, dim):
    return lax.broadcasted_iota(jnp.int32, shape, dim)


def one_hot(mask):
    return jnp.where(mask, 1.0, 0.0).astype(BF16)


def identity(size):
    return one_hot(iota((size, size), 0) == iota((size, size), 1))


def pick(fields, ids):
    slots = fields.shape[1]
    step = 512
    total = None
    for start in range(0, slots, step):
        chosen = one_hot(iota((step, ids.shape[1]), 0) + start == ids)
        part = dot(fields[:, start : start + step], chosen)
        total = part if total is None else total + part
    return total


def package(ensemble, value, var):
    members = ensemble.shape[0]
    centre = jnp.sum(ensemble, axis=0, keepdims=True) / members
    anomaly = ensemble - centre
    spread = jnp.sum(anomaly * anomaly, axis=0, keepdims=True) / (members - 1)
    gain = 1.0 / (spread + var)
    factor = 1.0 / (1.0 + jnp.sqrt(var * gain))
    coef_anom = factor * gain / (members - 1)
    coef_mean = gain * (value - centre) / (members - 1)
    return anomaly, coef_anom, coef_mean


def scale_tile(picked, members, value_row, mean_ref, anom_ref, taper_ref, colour, tile, new_mean_ref, scaled_ref):
    value = picked[value_row : value_row + 1]
    var = picked[value_row + 1 : value_row + 2]
    anomaly, coef_anom, coef_mean = package(picked[:members], value, var)
    basis = anomaly.astype(BF16)
    listed = basis.shape[1]
    coefs = jnp.concatenate([coef_anom, coef_mean, jnp.zeros((6, listed), F32)], axis=0).T
    taper = taper_ref[colour, tile].astype(F32)
    taper_anom = taper * coefs[:, 0:1]
    taper_mean = taper * coefs[:, 1:2]
    width = taper.shape[1]
    step = 2 * width
    for start in range(0, anom_ref.shape[2], step):
        projection = dot(basis, anom_ref[tile, :, start : start + step], ((0,), (0,)))
        for part in range(0, step, width):
            cells = slice(start + part, start + part + width)
            level = projection[:, part : part + width]
            scaled_ref[tile, :, cells] = (taper_anom * level).astype(BF16)
            shift = jnp.sum(taper_mean * level, axis=0, keepdims=True)
            new_mean_ref[tile : tile + 1, cells] = mean_ref[tile : tile + 1, cells] + shift
    return basis


def shift_tile(basis, mean_ref, anom_ref, tile, new_mean_ref, new_anom_ref, scaled_ref, width, change_ref):
    step = 2 * width
    for start in range(0, anom_ref.shape[2], step):
        cells = slice(start, start + step)
        old = anom_ref[tile, :, cells].astype(F32)
        new_anom = (old - dot(basis, scaled_ref[tile, :, cells])).astype(BF16)
        new_anom_ref[tile, :, cells] = new_anom
        if change_ref is not None:
            rise = new_mean_ref[tile : tile + 1, cells] - mean_ref[tile : tile + 1, cells]
            change = (new_anom.astype(F32) - old + rise).astype(BF16)
            for part in range(2):
                change_ref[start // width + part, :, tile * width : (tile + 1) * width] = change[
                    :, part * width : (part + 1) * width
                ]


def update_tiles(
    listed, table_ref, colour, members, value_row, mean_ref, anom_ref, taper_ref,
    new_mean_ref, new_anom_ref, scaled_ref, change_ref,
):
    bases = []
    length = taper_ref.shape[2]
    for tile in range(anom_ref.shape[0]):
        ids = table_ref[LISTS + colour : LISTS + colour + 1, tile * length : (tile + 1) * length]
        picked = pick(listed, ids)
        bases.append(
            scale_tile(
                picked, members, value_row, mean_ref, anom_ref, taper_ref, colour, tile, new_mean_ref, scaled_ref
            )
        )
    for tile, basis in enumerate(bases):
        shift_tile(
            basis, mean_ref, anom_ref, tile, new_mean_ref, new_anom_ref, scaled_ref, taper_ref.shape[3], change_ref
        )


def prepare_kernel(
    chips, tile_columns, prior_in, value_in, var_in, home_in, lists_in, mean_in,
    first_ref, second_ref, table_ref, mean_ref, crowded_ref, prior_ref, value_ref, var_ref, home_ref, lists_ref, sems,
):
    copies = [
        pltpu.make_async_copy(source, target, sems.at[i])
        for i, (source, target) in enumerate(
            (
                (prior_in, prior_ref), (value_in, value_ref), (var_in, var_ref), (home_in, home_ref), (lists_in, lists_ref),
                (mean_in, mean_ref),
            )
        )
    ]
    for copy in copies:
        copy.start()
    for copy in copies:
        copy.wait()
    _, width, members = prior_ref.shape
    row = iota((LANES, width), 0) - members
    value = value_ref[...].astype(F32)
    var = var_ref[...].astype(F32)
    tail = jnp.where(row == 0, value[0:1], 0.0)
    tail = jnp.where(row == 1, var[0:1], tail)
    tail = jnp.where(row == 2, value[1:2], tail)
    tail = jnp.where(row == 3, var[1:2], tail).astype(BF16)
    widen = one_hot(iota((members, LANES), 0) == iota((members, LANES), 1))
    first_ref[...] = (dot(prior_ref[0], widen) + dot(identity(width), tail, ((1,), (1,)))).astype(BF16)
    second_ref[...] = dot(prior_ref[1], widen).astype(BF16)
    colours, tiles, length = lists_ref.shape
    region = home_ref.shape[1]
    state, own_chip, core = lax.axis_index("state"), lax.axis_index("chip"), lax.axis_index("core")
    device_columns = tiles * tile_columns
    own = own_chip * 2 + core
    column = home_ref[...] - state * (chips * 2 * device_columns)
    device = jnp.zeros_like(column)
    for edge in range(1, chips * 2):
        device = device + jnp.where(column >= edge * device_columns, 1, 0)
    device = device.astype(F32)
    across = jnp.broadcast_to(device, (8, region)).T[:, 0:1]
    earlier = (across == device) & (iota((region, region), 0) < iota((region, region), 1))
    rank = jnp.sum(jnp.where(earlier, 1.0, 0.0), axis=0, keepdims=True)
    slot = (device * SLOTS + rank).astype(jnp.int32)
    table_ref[SLOT : SLOT + 1] = slot
    table_ref[MINE : MINE + 1] = slot - own * SLOTS
    table_ref[NEAR : NEAR + 1] = column - own * device_columns
    for colour in range(colours):
        for tile in range(tiles):
            table_ref[LISTS + colour : LISTS + colour + 1, tile * length : (tile + 1) * length] = (
                lists_ref[colour, tile : tile + 1] - (state - 1) * region
            )
    crowded_ref[0] = (jnp.max(rank) >= SLOTS).astype(jnp.int32)


def first_kernel(
    records_ref, table_ref, weight_ref, mean_ref, anom_ref, taper_ref,
    new_mean_ref, new_anom_ref, packed_ref, prior_ref, errors_ref, rows_ref, scaled_ref, change_ref,
):
    members = anom_ref.shape[1]
    _, dealt, _, width, _ = records_ref.shape
    chips = dealt // 2
    region = 2 * chips * width
    for chip in range(chips):
        for core in range(2):
            at = (chip * 2 + core) * width
            here = chip + (1 - core) * chips
            for part, block in enumerate(
                (
                    records_ref[0, chip, core], records_ref[core, here, 0],
                    records_ref[1, chips + chip, core], records_ref[core, here, 1],
                )
            ):
                rows_ref[part * region + at : part * region + at + width] = block
    turn = identity(LANES)
    fields = dot(turn, rows_ref[...], ((1,), (1,)))
    listed = fields[: members + 16, : 3 * region].astype(BF16)
    errors_ref[...] = listed[members:]
    update_tiles(
        listed, table_ref, 0, members, members, mean_ref, anom_ref, taper_ref,
        new_mean_ref, new_anom_ref, scaled_ref, change_ref,
    )
    home = table_ref[NEAR : NEAR + 1]
    columns = change_ref.shape[2]
    at_home = one_hot(iota((columns, region), 0) == home)
    prior = fields[:members, 3 * region :]
    increment = None
    for level in range(change_ref.shape[0]):
        part = dot(change_ref[level], at_home) * weight_ref[level : level + 1]
        increment = part if increment is None else increment + part
    inside = (home >= 0) & (home < columns)
    updated = jnp.where(inside, prior + increment, 0.0).astype(BF16)
    prior_ref[...] = updated
    lane = iota((LANES, region), 0)
    to_slot = one_hot(jnp.where(lane < SLOTS, lane, lane - SLOTS) == table_ref[MINE : MINE + 1])
    twice = dot(updated, to_slot, ((1,), (1,)))
    half = members // 2
    packed_ref[...] = jnp.where(iota((half, LANES), 1) < SLOTS, twice[:half], twice[half:]).astype(BF16)


def spread_kernel(packed_ref, table_ref, prior_ref):
    region = table_ref.shape[1]
    _, chips, half, _ = packed_ref.shape
    first = iota((half, LANES), 1) < SLOTS
    rows = iota((2 * SLOTS, region), 0)
    total = None
    for chip in range(chips):
        low, high = packed_ref[0, chip].astype(F32), packed_ref[1, chip].astype(F32)
        upper = jnp.where(first, low, pltpu.roll(high, SLOTS, 1))
        lower = jnp.where(first, pltpu.roll(low, SLOTS, 1), high)
        ensemble = jnp.concatenate([upper, lower], axis=0).astype(BF16)
        part = dot(ensemble, one_hot(rows + chip * 2 * SLOTS == table_ref[SLOT : SLOT + 1]))
        total = part if total is None else total + part
    prior_ref[...] = total.astype(BF16)


def second_kernel(
    own_ref, beside_ref, errors_ref, table_ref, mean_ref, anom_ref, taper_ref,
    new_mean_ref, new_anom_ref, scaled_ref,
):
    members = anom_ref.shape[1]
    ensemble = jnp.concatenate([beside_ref[0], own_ref[...], beside_ref[1]], axis=1)
    listed = jnp.concatenate([ensemble, errors_ref[...]], axis=0)
    update_tiles(
        listed, table_ref, 1, members, members + 2, mean_ref, anom_ref, taper_ref,
        new_mean_ref, new_anom_ref, scaled_ref, None,
    )


def beside(rows, chips, states):
    at = lambda state, chip, core: (state * chips + chip) * 2 + core
    groups = [[at(s, c, 1), at(s + 1, c, 0)] for s in range(states - 1) for c in range(chips)]
    for state, core in ((0, 0), (states - 1, 1)):
        groups += [[at(state, c, core), at(state, c + 1, core)] for c in range(0, chips, 2)]
    swapped = lax.all_gather(rows, ("state", "chip", "core"), axis_index_groups=groups)
    partner = jnp.where(lax.axis_index("core") == 1, swapped[1], swapped[0])
    return lax.all_gather(partner, "core")


def across_two(first, second, crowded, chips, states):
    at = lambda state, chip, core: (state * chips + chip) * 2 + core
    groups = [
        [at(s, c, 1) for c in range(chips)] + [at((s + 1) % states, c, 0) for c in range(chips)] for s in range(states)
    ]
    pair = lax.all_gather(first, "core")
    own = jnp.stack([first, second])
    low = (lax.iota(jnp.int32, 2 * chips) < chips) == (lax.axis_index("core") == 1)
    sent = jnp.where(low[:, None, None, None], own[None], pair[None])
    dealt = lax.all_to_all(sent, ("state", "chip", "core"), 0, 0, axis_index_groups=groups)
    return lax.optimization_barrier((lax.all_gather(dealt, "core"), crowded))


def local(state_mean, state_anom, obs_prior, obs_value, obs_var, obs_weight, obs_home, tile_obs, taper):
    tiles, members, cells = state_anom.shape
    tile_width = taper.shape[3]
    chips, states = lax.axis_size("chip"), lax.axis_size("state")
    width = obs_prior.shape[2]
    region = 2 * chips * width
    raw = (jnp.swapaxes(obs_prior, 1, 2), obs_value, obs_var, obs_home[None], tile_obs, state_mean)
    block = jax.ShapeDtypeStruct((width, LANES), BF16)
    first, second, table, mean, crowded = pl.pallas_call(
        functools.partial(prepare_kernel, chips, tile_width),
        out_shape=(
            block,
            block,
            jax.ShapeDtypeStruct((8, region), jnp.int32),
            jax.ShapeDtypeStruct(state_mean.shape, state_mean.dtype),
            pltpu.SMEM((1,), jnp.int32),
        ),
        in_specs=[pl.BlockSpec(memory_space=pltpu.HBM)] * len(raw),
        out_specs=(VMEM, VMEM, VMEM, VMEM, SMEM),
        scratch_shapes=[pltpu.VMEM(a.shape, a.dtype) for a in raw[:-1]] + [pltpu.SemaphoreType.DMA((len(raw),))],
        compiler_params=SMALL,
        name="prepare",
    )(*[pltpu.with_memory_space_constraint(a, pltpu.HBM) for a in raw])
    records, crowded = across_two(first, second, crowded, chips, states)

    state_shapes = (
        jax.ShapeDtypeStruct(state_mean.shape, state_mean.dtype),
        jax.ShapeDtypeStruct(state_anom.shape, state_anom.dtype),
    )
    scaled = pltpu.VMEM((tiles, tile_obs.shape[2], cells), BF16)
    prior_shape = jax.ShapeDtypeStruct((members, region), BF16)
    new_mean, new_anom, packed, prior, errors = pl.pallas_call(
        first_kernel,
        out_shape=state_shapes
        + (
            jax.ShapeDtypeStruct((members // 2, LANES), BF16),
            prior_shape,
            jax.ShapeDtypeStruct((16, 3 * region), BF16),
        ),
        in_specs=[VMEM] * 6,
        out_specs=(VMEM,) * 5,
        scratch_shapes=[
            pltpu.VMEM((4 * region, LANES), BF16),
            scaled,
            pltpu.VMEM((cells // tile_width, members, tiles * tile_width), BF16),
        ],
        compiler_params=LARGE,
        name="first",
    )(records, table, obs_weight, mean, state_anom, taper)

    def to_row(part):
        return lax.all_to_all(jnp.broadcast_to(part[None], (chips,) + part.shape), "chip", 0, 0)

    def by_slot(packed, prior, table):
        return pl.pallas_call(
            spread_kernel,
            out_shape=prior_shape,
            in_specs=[VMEM] * 2,
            out_specs=VMEM,
            compiler_params=SMALL,
            name="spread",
        )(lax.all_gather(to_row(packed), "core"), table)

    def whole(packed, prior, table):
        both = lax.all_gather(prior, "core")
        return jnp.sum(to_row(both[0] + both[1]), axis=0, dtype=BF16)

    own = lax.cond(crowded[0] == 0, by_slot, whole, packed, prior, table)
    sides = beside(own, chips, states)

    return pl.pallas_call(
        second_kernel,
        out_shape=state_shapes,
        in_specs=[VMEM] * 7,
        out_specs=(VMEM,) * 2,
        scratch_shapes=[scaled],
        compiler_params=LARGE,
        name="second",
    )(own, sides, errors, table, new_mean, new_anom, taper)


def solution(mesh):
    states, columns = mesh.shape["state"], mesh.shape["obs"]
    fine = Mesh(mesh.devices.reshape(states, columns // 2, 2), ("state", "chip", "core"))
    every = ("state", "chip", "core")
    in_specs = (
        P(every, None),
        P(every, None, None),
        P(None, None, every),
        P(None, every),
        P(None, every),
        P(None, "state"),
        P("state"),
        P(None, every, None),
        P(None, every, None, None),
    )
    out_specs = (P(every, None), P(every, None, None))
    return jax.shard_map(local, mesh=fine, in_specs=in_specs, out_specs=out_specs, check_vma=False)
```

```python
import functools

import jax
import jax.numpy as jnp
from jax import lax
from jax.experimental import pallas as pl
from jax.experimental.pallas import tpu as pltpu
from jax.sharding import Mesh
from jax.sharding import PartitionSpec as P

F32 = jnp.float32
BF16 = jnp.bfloat16
LANES = 128
SLOTS = 64
KEPT = 84
SLOT, MINE, NEAR, LISTS = 0, 1, 2, 3
VMEM = pl.BlockSpec(memory_space=pltpu.VMEM)
SMEM = pl.BlockSpec(memory_space=pltpu.SMEM)
SMALL = pltpu.CompilerParams(vmem_limit_bytes=8 * 1024 * 1024)
LARGE = pltpu.CompilerParams(vmem_limit_bytes=24 * 1024 * 1024)


def dot(a, b, contract=((1,), (0,))):
    return lax.dot_general(a, b, (contract, ((), ())), preferred_element_type=F32)


def iota(shape, dim):
    return lax.broadcasted_iota(jnp.int32, shape, dim)


def one_hot(mask):
    return jnp.where(mask, 1.0, 0.0).astype(BF16)


def identity(size):
    return one_hot(iota((size, size), 0) == iota((size, size), 1))


def pick(fields, ids):
    slots = fields.shape[1]
    step = 512
    total = None
    for start in range(0, slots, step):
        chosen = one_hot(iota((step, ids.shape[1]), 0) + start == ids)
        part = dot(fields[:, start : start + step], chosen)
        total = part if total is None else total + part
    return total


def package(ensemble, value, var):
    members = ensemble.shape[0]
    centre = jnp.sum(ensemble, axis=0, keepdims=True) / members
    anomaly = ensemble - centre
    spread = jnp.sum(anomaly * anomaly, axis=0, keepdims=True) / (members - 1)
    gain = 1.0 / (spread + var)
    factor = 1.0 / (1.0 + jnp.sqrt(var * gain))
    coef_anom = factor * gain / (members - 1)
    coef_mean = gain * (value - centre) / (members - 1)
    return anomaly, coef_anom, coef_mean


def scale_tile(basis, coefs, mean_ref, anom_ref, taper, tile, new_mean_ref, scaled_ref):
    taper = taper.astype(F32)
    taper_anom = taper * coefs[:, 0:1]
    taper_mean = taper * coefs[:, 1:2]
    width = taper.shape[1]
    step = 2 * width
    for start in range(0, anom_ref.shape[2], step):
        projection = dot(basis, anom_ref[tile, :, start : start + step], ((0,), (0,)))
        for part in range(0, step, width):
            cells = slice(start + part, start + part + width)
            level = projection[:, part : part + width]
            scaled_ref[tile, :, cells] = (taper_anom * level).astype(BF16)
            shift = jnp.sum(taper_mean * level, axis=0, keepdims=True)
            new_mean_ref[tile : tile + 1, cells] = mean_ref[tile : tile + 1, cells] + shift


def shift_tile(basis, mean_ref, anom_ref, tile, new_mean_ref, new_anom_ref, scaled_ref, width, change_ref):
    step = 2 * width
    for start in range(0, anom_ref.shape[2], step):
        cells = slice(start, start + step)
        old = anom_ref[tile, :, cells].astype(F32)
        new_anom = (old - dot(basis, scaled_ref[tile, :, cells])).astype(BF16)
        new_anom_ref[tile, :, cells] = new_anom
        if change_ref is not None:
            rise = new_mean_ref[tile : tile + 1, cells] - mean_ref[tile : tile + 1, cells]
            change = (new_anom.astype(F32) - old + rise).astype(BF16)
            for part in range(2):
                change_ref[start // width + part, :, tile * width : (tile + 1) * width] = change[
                    :, part * width : (part + 1) * width
                ]


def update_tiles(
    listed, table_ref, colour, members, value_row, mean_ref, anom_ref, taper_ref,
    new_mean_ref, new_anom_ref, scaled_ref, change_ref,
):
    tiles, length = taper_ref.shape[1], taper_ref.shape[2]
    picked = pick(listed, table_ref[LISTS + colour : LISTS + colour + 1])
    anomaly, coef_anom, coef_mean = package(
        picked[:members], picked[value_row : value_row + 1], picked[value_row + 1 : value_row + 2]
    )
    basis = anomaly.astype(BF16)
    coefs = jnp.concatenate([coef_anom, coef_mean, jnp.zeros((6, tiles * length), F32)], axis=0).T
    for tile in range(tiles):
        own = slice(tile * length, (tile + 1) * length)
        scale_tile(
            basis[:, own], coefs[own], mean_ref, anom_ref, taper_ref[colour, tile], tile, new_mean_ref, scaled_ref
        )
    for tile in range(tiles):
        own = slice(tile * length, (tile + 1) * length)
        shift_tile(
            basis[:, own], mean_ref, anom_ref, tile, new_mean_ref, new_anom_ref, scaled_ref, taper_ref.shape[3],
            change_ref,
        )


def fold(block, other):
    other = pltpu.roll(other, KEPT, 1)
    lane = iota(block.shape, 1)
    half = block.shape[0] // 2
    beneath = jnp.where(lane[:half] < LANES // 2, other[:half], pltpu.roll(other[half:], LANES // 2, 1))
    return jnp.concatenate([jnp.where(lane < KEPT, block, other), beneath], axis=0).astype(BF16)


def unfold(folded):
    folded = folded.astype(F32)
    width = folded.shape[0] * 2 // 3
    beneath = folded[width:]
    other = jnp.concatenate([beneath, pltpu.roll(beneath, LANES // 2, 1)], axis=0)
    lane = iota((width, LANES), 1)
    return pltpu.roll(jnp.where(lane < KEPT, other, folded[:width]), LANES - KEPT, 1).astype(BF16)


def prepare_kernel(
    chips, tile_columns, prior_in, value_in, var_in, home_in, lists_in, mean_in,
    own_ref, pair_ref, table_ref, mean_ref, crowded_ref, prior_ref, value_ref, var_ref, home_ref, lists_ref, sems,
):
    copies = [
        pltpu.make_async_copy(source, target, sems.at[i])
        for i, (source, target) in enumerate(
            (
                (prior_in, prior_ref), (value_in, value_ref), (var_in, var_ref), (home_in, home_ref), (lists_in, lists_ref),
                (mean_in, mean_ref),
            )
        )
    ]
    for copy in copies:
        copy.start()
    for copy in copies:
        copy.wait()
    _, width, members = prior_ref.shape
    row = iota((LANES, width), 0) - members
    value = value_ref[...].astype(F32)
    var = var_ref[...].astype(F32)
    tail = jnp.where(row == 0, value[0:1], 0.0)
    tail = jnp.where(row == 1, var[0:1], tail)
    tail = jnp.where(row == 2, value[1:2], tail)
    tail = jnp.where(row == 3, var[1:2], tail).astype(BF16)
    widen = one_hot(iota((members, LANES), 0) == iota((members, LANES), 1))
    first = dot(prior_ref[0], widen) + dot(identity(width), tail, ((1,), (1,)))
    second = dot(prior_ref[1], widen)
    none = jnp.zeros_like(first)
    on_first = lax.axis_index("core") == 0
    own_ref[...] = fold(first, second)
    pair_ref[...] = fold(jnp.where(on_first, first, none), jnp.where(on_first, none, first))
    colours, tiles, length = lists_ref.shape
    region = home_ref.shape[1]
    state, own_chip, core = lax.axis_index("state"), lax.axis_index("chip"), lax.axis_index("core")
    device_columns = tiles * tile_columns
    own = own_chip * 2 + core
    column = home_ref[...] - state * (chips * 2 * device_columns)
    device = jnp.zeros_like(column)
    for edge in range(1, chips * 2):
        device = device + jnp.where(column >= edge * device_columns, 1, 0)
    device = device.astype(F32)
    across = jnp.broadcast_to(device, (8, region)).T[:, 0:1]
    earlier = (across == device) & (iota((region, region), 0) < iota((region, region), 1))
    rank = jnp.sum(jnp.where(earlier, 1.0, 0.0), axis=0, keepdims=True)
    slot = (device * SLOTS + rank).astype(jnp.int32)
    table_ref[SLOT : SLOT + 1] = slot
    table_ref[MINE : MINE + 1] = slot - own * SLOTS
    table_ref[NEAR : NEAR + 1] = column - own * device_columns
    for colour in range(colours):
        for tile in range(tiles):
            table_ref[LISTS + colour : LISTS + colour + 1, tile * length : (tile + 1) * length] = (
                lists_ref[colour, tile : tile + 1] - (state - 1) * region
            )
    crowded_ref[0] = (jnp.max(rank) >= SLOTS).astype(jnp.int32)


def first_kernel(
    records_ref, table_ref, weight_ref, mean_ref, anom_ref, taper_ref,
    new_mean_ref, new_anom_ref, packed_ref, prior_ref, errors_ref, rows_ref, scaled_ref, change_ref,
):
    members = anom_ref.shape[1]
    _, dealt, height, _ = records_ref.shape
    chips, width = dealt // 2, height * 2 // 3
    region = 2 * chips * width
    for chip in range(chips):
        at = chip * 2 * width
        for side, part in ((0, 0), (1, 2)):
            folded = records_ref[side, side * chips + chip]
            rows_ref[part * region + at : part * region + at + width] = folded[:width]
            rows_ref[part * region + at + width : part * region + at + 2 * width] = unfold(folded)
        for core in range(2):
            folded = records_ref[core, chip + (1 - core) * chips]
            here = at + core * width
            rows_ref[region + here : region + here + width] = folded[:width]
            rows_ref[3 * region + here : 3 * region + here + width] = unfold(folded)
    turn = identity(LANES)
    fields = dot(turn, rows_ref[...], ((1,), (1,)))
    listed = fields[: members + 16, : 3 * region].astype(BF16)
    errors_ref[...] = listed[members:]
    update_tiles(
        listed, table_ref, 0, members, members, mean_ref, anom_ref, taper_ref,
        new_mean_ref, new_anom_ref, scaled_ref, change_ref,
    )
    home = table_ref[NEAR : NEAR + 1]
    columns = change_ref.shape[2]
    at_home = one_hot(iota((columns, region), 0) == home)
    prior = fields[:members, 3 * region :]
    increment = None
    for level in range(change_ref.shape[0]):
        part = dot(change_ref[level], at_home) * weight_ref[level : level + 1]
        increment = part if increment is None else increment + part
    inside = (home >= 0) & (home < columns)
    updated = jnp.where(inside, prior + increment, 0.0).astype(BF16)
    prior_ref[...] = updated
    lane = iota((LANES, region), 0)
    to_slot = one_hot(jnp.where(lane < SLOTS, lane, lane - SLOTS) == table_ref[MINE : MINE + 1])
    twice = dot(updated, to_slot, ((1,), (1,)))
    half = members // 2
    packed_ref[...] = jnp.where(iota((half, LANES), 1) < SLOTS, twice[:half], twice[half:]).astype(BF16)


def spread_kernel(packed_ref, table_ref, prior_ref):
    region = table_ref.shape[1]
    _, chips, half, _ = packed_ref.shape
    first = iota((half, LANES), 1) < SLOTS
    rows = iota((2 * SLOTS, region), 0)
    total = None
    for chip in range(chips):
        low, high = packed_ref[0, chip].astype(F32), packed_ref[1, chip].astype(F32)
        upper = jnp.where(first, low, pltpu.roll(high, SLOTS, 1))
        lower = jnp.where(first, pltpu.roll(low, SLOTS, 1), high)
        ensemble = jnp.concatenate([upper, lower], axis=0).astype(BF16)
        part = dot(ensemble, one_hot(rows + chip * 2 * SLOTS == table_ref[SLOT : SLOT + 1]))
        total = part if total is None else total + part
    prior_ref[...] = total.astype(BF16)


def second_kernel(
    own_ref, beside_ref, errors_ref, table_ref, mean_ref, anom_ref, taper_ref,
    new_mean_ref, new_anom_ref, scaled_ref,
):
    members = anom_ref.shape[1]
    ensemble = jnp.concatenate([beside_ref[0], own_ref[...], beside_ref[1]], axis=1)
    listed = jnp.concatenate([ensemble, errors_ref[...]], axis=0)
    update_tiles(
        listed, table_ref, 1, members, members + 2, mean_ref, anom_ref, taper_ref,
        new_mean_ref, new_anom_ref, scaled_ref, None,
    )


def beside(rows, chips, states):
    at = lambda state, chip, core: (state * chips + chip) * 2 + core
    groups = [[at(s, c, 1), at(s + 1, c, 0)] for s in range(states - 1) for c in range(chips)]
    for state, core in ((0, 0), (states - 1, 1)):
        groups += [[at(state, c, core), at(state, c + 1, core)] for c in range(0, chips, 2)]
    swapped = lax.all_gather(rows, ("state", "chip", "core"), axis_index_groups=groups)
    partner = jnp.where(lax.axis_index("core") == 1, swapped[1], swapped[0])
    return lax.all_gather(partner, "core")


def across_two(own, pair, crowded, chips, states):
    at = lambda state, chip, core: (state * chips + chip) * 2 + core
    groups = [
        [at(s, c, 1) for c in range(chips)] + [at((s + 1) % states, c, 0) for c in range(chips)] for s in range(states)
    ]
    pair = lax.all_gather(pair, "core")
    low = (lax.iota(jnp.int32, 2 * chips) < chips) == (lax.axis_index("core") == 1)
    sent = jnp.where(low[:, None, None], own[None], (pair[0] + pair[1])[None])
    dealt = lax.all_to_all(sent, ("state", "chip", "core"), 0, 0, axis_index_groups=groups)
    return lax.optimization_barrier((lax.all_gather(dealt, "core"), crowded))


def local(state_mean, state_anom, obs_prior, obs_value, obs_var, obs_weight, obs_home, tile_obs, taper):
    tiles, members, cells = state_anom.shape
    tile_width = taper.shape[3]
    chips, states = lax.axis_size("chip"), lax.axis_size("state")
    width = obs_prior.shape[2]
    region = 2 * chips * width
    raw = (jnp.swapaxes(obs_prior, 1, 2), obs_value, obs_var, obs_home[None], tile_obs, state_mean)
    block = jax.ShapeDtypeStruct((width * 3 // 2, LANES), BF16)
    own, pair, table, mean, crowded = pl.pallas_call(
        functools.partial(prepare_kernel, chips, tile_width),
        out_shape=(
            block,
            block,
            jax.ShapeDtypeStruct((8, region), jnp.int32),
            jax.ShapeDtypeStruct(state_mean.shape, state_mean.dtype),
            pltpu.SMEM((1,), jnp.int32),
        ),
        in_specs=[pl.BlockSpec(memory_space=pltpu.HBM)] * len(raw),
        out_specs=(VMEM, VMEM, VMEM, VMEM, SMEM),
        scratch_shapes=[pltpu.VMEM(a.shape, a.dtype) for a in raw[:-1]] + [pltpu.SemaphoreType.DMA((len(raw),))],
        compiler_params=SMALL,
        name="prepare",
    )(*[pltpu.with_memory_space_constraint(a, pltpu.HBM) for a in raw])
    records, crowded = across_two(own, pair, crowded, chips, states)

    state_shapes = (
        jax.ShapeDtypeStruct(state_mean.shape, state_mean.dtype),
        jax.ShapeDtypeStruct(state_anom.shape, state_anom.dtype),
    )
    scaled = pltpu.VMEM((tiles, tile_obs.shape[2], cells), BF16)
    prior_shape = jax.ShapeDtypeStruct((members, region), BF16)
    new_mean, new_anom, packed, prior, errors = pl.pallas_call(
        first_kernel,
        out_shape=state_shapes
        + (
            jax.ShapeDtypeStruct((members // 2, LANES), BF16),
            prior_shape,
            jax.ShapeDtypeStruct((16, 3 * region), BF16),
        ),
        in_specs=[VMEM] * 6,
        out_specs=(VMEM,) * 5,
        scratch_shapes=[
            pltpu.VMEM((4 * region, LANES), BF16),
            scaled,
            pltpu.VMEM((cells // tile_width, members, tiles * tile_width), BF16),
        ],
        compiler_params=LARGE,
        name="first",
    )(records, table, obs_weight, mean, state_anom, taper)

    def to_row(part):
        return lax.all_to_all(jnp.broadcast_to(part[None], (chips,) + part.shape), "chip", 0, 0)

    def by_slot(packed, prior, table):
        return pl.pallas_call(
            spread_kernel,
            out_shape=prior_shape,
            in_specs=[VMEM] * 2,
            out_specs=VMEM,
            compiler_params=SMALL,
            name="spread",
        )(lax.all_gather(to_row(packed), "core"), table)

    def whole(packed, prior, table):
        both = lax.all_gather(prior, "core")
        return jnp.sum(to_row(both[0] + both[1]), axis=0, dtype=BF16)

    prior_row = lax.cond(crowded[0] == 0, by_slot, whole, packed, prior, table)
    sides = beside(prior_row, chips, states)

    return pl.pallas_call(
        second_kernel,
        out_shape=state_shapes,
        in_specs=[VMEM] * 7,
        out_specs=(VMEM,) * 2,
        scratch_shapes=[scaled],
        compiler_params=LARGE,
        name="second",
    )(prior_row, sides, errors, table, new_mean, new_anom, taper)


def solution(mesh):
    states, columns = mesh.shape["state"], mesh.shape["obs"]
    fine = Mesh(mesh.devices.reshape(states, columns // 2, 2), ("state", "chip", "core"))
    every = ("state", "chip", "core")
    in_specs = (
        P(every, None),
        P(every, None, None),
        P(None, None, every),
        P(None, every),
        P(None, every),
        P(None, "state"),
        P("state"),
        P(None, every, None),
        P(None, every, None, None),
    )
    out_specs = (P(every, None), P(every, None, None))
    return jax.shard_map(local, mesh=fine, in_specs=in_specs, out_specs=out_specs, check_vma=False)
```

```python
import functools

import jax
import jax.numpy as jnp
from jax import lax
from jax.experimental import pallas as pl
from jax.experimental.pallas import tpu as pltpu
from jax.sharding import Mesh
from jax.sharding import PartitionSpec as P

F32 = jnp.float32
BF16 = jnp.bfloat16
LANES = 128
SLOTS = 64
KEPT = 84
SLOT, MINE, NEAR, LISTS = 0, 1, 2, 3
VMEM = pl.BlockSpec(memory_space=pltpu.VMEM)
SMEM = pl.BlockSpec(memory_space=pltpu.SMEM)
SMALL = pltpu.CompilerParams(vmem_limit_bytes=8 * 1024 * 1024)
LARGE = pltpu.CompilerParams(vmem_limit_bytes=24 * 1024 * 1024)


def dot(a, b, contract=((1,), (0,))):
    return lax.dot_general(a, b, (contract, ((), ())), preferred_element_type=F32)


def iota(shape, dim):
    return lax.broadcasted_iota(jnp.int32, shape, dim)


def one_hot(mask):
    return jnp.where(mask, 1.0, 0.0).astype(BF16)


def identity(size):
    return one_hot(iota((size, size), 0) == iota((size, size), 1))


def pick(fields, ids):
    slots = fields.shape[1]
    step = 512
    total = None
    for start in range(0, slots, step):
        chosen = one_hot(iota((step, ids.shape[1]), 0) + start == ids)
        part = dot(fields[:, start : start + step], chosen)
        total = part if total is None else total + part
    return total


def package(ensemble, value, var):
    members = ensemble.shape[0]
    centre = jnp.sum(ensemble, axis=0, keepdims=True) / members
    anomaly = ensemble - centre
    spread = jnp.sum(anomaly * anomaly, axis=0, keepdims=True) / (members - 1)
    gain = 1.0 / (spread + var)
    factor = 1.0 / (1.0 + jnp.sqrt(var * gain))
    coef_anom = factor * gain / (members - 1)
    coef_mean = gain * (value - centre) / (members - 1)
    return anomaly, coef_anom, coef_mean


def scale_tile(basis, coefs, mean_ref, anom_ref, taper, tile, new_mean_ref, scaled_ref):
    taper = taper.astype(F32)
    taper_anom = taper * coefs[:, 0:1]
    taper_mean = taper * coefs[:, 1:2]
    width = taper.shape[1]
    step = 2 * width
    for start in range(0, anom_ref.shape[2], step):
        projection = dot(basis, anom_ref[tile, :, start : start + step], ((0,), (0,)))
        for part in range(0, step, width):
            cells = slice(start + part, start + part + width)
            level = projection[:, part : part + width]
            scaled_ref[tile, :, cells] = (taper_anom * level).astype(BF16)
            shift = jnp.sum(taper_mean * level, axis=0, keepdims=True)
            new_mean_ref[tile : tile + 1, cells] = mean_ref[tile : tile + 1, cells] + shift


def shift_tile(basis, mean_ref, anom_ref, tile, new_mean_ref, new_anom_ref, scaled_ref, width, change_ref):
    step = 2 * width
    for start in range(0, anom_ref.shape[2], step):
        cells = slice(start, start + step)
        old = anom_ref[tile, :, cells].astype(F32)
        new_anom = (old - dot(basis, scaled_ref[tile, :, cells])).astype(BF16)
        new_anom_ref[tile, :, cells] = new_anom
        if change_ref is not None:
            rise = new_mean_ref[tile : tile + 1, cells] - mean_ref[tile : tile + 1, cells]
            high = rise.astype(BF16).astype(F32)
            middle = (rise - high).astype(BF16).astype(F32)
            row = iota((16, step), 0)
            rises = jnp.where(row == 0, high, jnp.where(row == 1, middle, jnp.where(row == 2, rise - high - middle, 0.0)))
            stack = (new_anom, anom_ref[tile, :, cells], rises.astype(BF16))
            for part in range(2):
                at = 0
                for values in stack:
                    change_ref[start // width + part, at : at + values.shape[0], tile * width : (tile + 1) * width] = values[
                        :, part * width : (part + 1) * width
                    ]
                    at += values.shape[0]


def update_tiles(
    listed, table_ref, colour, members, value_row, mean_ref, anom_ref, taper_ref,
    new_mean_ref, new_anom_ref, scaled_ref, change_ref,
):
    tiles, length = taper_ref.shape[1], taper_ref.shape[2]
    picked = pick(listed, table_ref[LISTS + colour : LISTS + colour + 1])
    anomaly, coef_anom, coef_mean = package(
        picked[:members], picked[value_row : value_row + 1], picked[value_row + 1 : value_row + 2]
    )
    basis = anomaly.astype(BF16)
    coefs = jnp.concatenate([coef_anom, coef_mean, jnp.zeros((6, tiles * length), F32)], axis=0).T
    for tile in range(tiles):
        own = slice(tile * length, (tile + 1) * length)
        scale_tile(
            basis[:, own], coefs[own], mean_ref, anom_ref, taper_ref[colour, tile], tile, new_mean_ref, scaled_ref
        )
    for tile in range(tiles):
        own = slice(tile * length, (tile + 1) * length)
        shift_tile(
            basis[:, own], mean_ref, anom_ref, tile, new_mean_ref, new_anom_ref, scaled_ref, taper_ref.shape[3],
            change_ref,
        )


def fold(block, other):
    other = pltpu.roll(other, KEPT, 1)
    lane = iota(block.shape, 1)
    half = block.shape[0] // 2
    beneath = jnp.where(lane[:half] < LANES // 2, other[:half], pltpu.roll(other[half:], LANES // 2, 1))
    return jnp.concatenate([jnp.where(lane < KEPT, block, other), beneath], axis=0).astype(BF16)


def unfold(folded):
    folded = folded.astype(F32)
    width = folded.shape[0] * 2 // 3
    beneath = folded[width:]
    other = jnp.concatenate([beneath, pltpu.roll(beneath, LANES // 2, 1)], axis=0)
    return jnp.where(iota((width, LANES), 1) < KEPT, other, folded[:width]).astype(BF16)


def prepare_kernel(
    chips, tile_columns, prior_in, value_in, var_in, home_in, lists_in, mean_in,
    own_ref, pair_ref, table_ref, mean_ref, crowded_ref, prior_ref, value_ref, var_ref, home_ref, lists_ref, sems,
):
    copies = [
        pltpu.make_async_copy(source, target, sems.at[i])
        for i, (source, target) in enumerate(
            (
                (prior_in, prior_ref), (value_in, value_ref), (var_in, var_ref), (home_in, home_ref), (lists_in, lists_ref),
                (mean_in, mean_ref),
            )
        )
    ]
    for copy in copies:
        copy.start()
    for copy in copies:
        copy.wait()
    _, width, members = prior_ref.shape
    row = iota((LANES, width), 0) - members
    value = value_ref[...].astype(F32)
    var = var_ref[...].astype(F32)
    tail = jnp.where(row == 0, value[0:1], 0.0)
    tail = jnp.where(row == 1, var[0:1], tail)
    tail = jnp.where(row == 2, value[1:2], tail)
    tail = jnp.where(row == 3, var[1:2], tail).astype(BF16)
    widen = one_hot(iota((members, LANES), 0) == iota((members, LANES), 1))
    first = dot(prior_ref[0], widen) + dot(identity(width), tail, ((1,), (1,)))
    second = dot(prior_ref[1], widen)
    none = jnp.zeros_like(first)
    on_first = lax.axis_index("core") == 0
    own_ref[...] = fold(first, second)
    pair_ref[...] = fold(jnp.where(on_first, first, none), jnp.where(on_first, none, first))
    colours, tiles, length = lists_ref.shape
    region = home_ref.shape[1]
    state, own_chip, core = lax.axis_index("state"), lax.axis_index("chip"), lax.axis_index("core")
    device_columns = tiles * tile_columns
    own = own_chip * 2 + core
    column = home_ref[...] - state * (chips * 2 * device_columns)
    first_column = iota((2 * chips, region), 0) * device_columns
    at_home = (column >= first_column) & (column < first_column + device_columns)
    at_home = jnp.where(at_home, 1.0, 0.0)
    earlier = one_hot(iota((LANES, LANES), 0) < iota((LANES, LANES), 1))
    ranks, before = [], jnp.zeros((2 * chips, 1), F32)
    for start in range(0, region, LANES):
        some = at_home[:, start : start + LANES]
        ranks.append(jnp.sum(some * (dot(some.astype(BF16), earlier) + before), axis=0, keepdims=True))
        before = before + jnp.sum(some, axis=1, keepdims=True)
    rank = jnp.concatenate(ranks, axis=1)
    device = jnp.sum(at_home * iota((2 * chips, region), 0).astype(F32), axis=0, keepdims=True)
    slot = (device * SLOTS + rank).astype(jnp.int32)
    table_ref[SLOT : SLOT + 1] = slot
    table_ref[MINE : MINE + 1] = slot - own * SLOTS
    table_ref[NEAR : NEAR + 1] = column - own * device_columns
    for colour in range(colours):
        for tile in range(tiles):
            table_ref[LISTS + colour : LISTS + colour + 1, tile * length : (tile + 1) * length] = (
                lists_ref[colour, tile : tile + 1] - (state - 1) * region
            )
    crowded_ref[0] = (jnp.max(rank) >= SLOTS).astype(jnp.int32)


def first_kernel(
    records_ref, table_ref, weight_ref, mean_ref, anom_ref, taper_ref,
    new_mean_ref, new_anom_ref, packed_ref, prior_ref, errors_ref, rows_ref, scaled_ref, change_ref,
):
    members = anom_ref.shape[1]
    _, dealt, height, _ = records_ref.shape
    chips, width = dealt // 2, height * 2 // 3
    region = 2 * chips * width
    for chip in range(chips):
        at = chip * 2 * width
        for side, part in ((0, 0), (1, 2)):
            folded = records_ref[side, side * chips + chip]
            rows_ref[part * region + at : part * region + at + width] = folded[:width]
            rows_ref[part * region + at + width : part * region + at + 2 * width] = unfold(folded)
        for core in range(2):
            folded = records_ref[core, chip + (1 - core) * chips]
            here = at + core * width
            rows_ref[region + here : region + here + width] = folded[:width]
            rows_ref[3 * region + here : 3 * region + here + width] = unfold(folded)
    count = members + 16
    field, lane = iota((count, LANES), 0), iota((count, LANES), 1)
    plain = one_hot(field == lane)
    turned = one_hot(jnp.where(field < LANES - KEPT, field + KEPT, field + KEPT - LANES) == lane)
    both = jnp.concatenate([plain, turned], axis=0)
    on_first = jnp.bitwise_and(iota((count, region), 1), 2 * width - 1) < width
    listed = []
    for part in range(3):
        rows = rows_ref[part * region : (part + 1) * region]
        if part == 1:
            listed.append(dot(plain, rows, ((1,), (1,))).astype(BF16))
        else:
            fields = dot(both, rows, ((1,), (1,)))
            listed.append(jnp.where(on_first, fields[:count], fields[count:]).astype(BF16))
    listed = jnp.concatenate(listed, axis=1)
    prior = dot(turned[:members], rows_ref[3 * region :], ((1,), (1,)))
    errors_ref[...] = listed[members:]
    update_tiles(
        listed, table_ref, 0, members, members, mean_ref, anom_ref, taper_ref,
        new_mean_ref, new_anom_ref, scaled_ref, change_ref,
    )
    home = table_ref[NEAR : NEAR + 1]
    columns = change_ref.shape[2]
    at_home = one_hot(iota((columns, region), 0) == home)
    increment = None
    for level in range(change_ref.shape[0]):
        chosen = dot(change_ref[level], at_home)
        rise = chosen[2 * members : 2 * members + 1] + chosen[2 * members + 1 : 2 * members + 2]
        rise = rise + chosen[2 * members + 2 : 2 * members + 3]
        part = (chosen[:members] - chosen[members : 2 * members] + rise) * weight_ref[level : level + 1]
        increment = part if increment is None else increment + part
    inside = (home >= 0) & (home < columns)
    updated = jnp.where(inside, prior + increment, 0.0).astype(BF16)
    prior_ref[...] = updated
    lane = iota((LANES, region), 0)
    to_slot = one_hot(jnp.where(lane < SLOTS, lane, lane - SLOTS) == table_ref[MINE : MINE + 1])
    twice = dot(updated, to_slot, ((1,), (1,)))
    half = members // 2
    packed_ref[...] = jnp.where(iota((half, LANES), 1) < SLOTS, twice[:half], twice[half:]).astype(BF16)


def spread_kernel(packed_ref, table_ref, prior_ref):
    region = table_ref.shape[1]
    _, chips, half, _ = packed_ref.shape
    first = iota((half, LANES), 1) < SLOTS
    rows = iota((2 * SLOTS, region), 0)
    total = None
    for chip in range(chips):
        low, high = packed_ref[0, chip].astype(F32), packed_ref[1, chip].astype(F32)
        upper = jnp.where(first, low, pltpu.roll(high, SLOTS, 1))
        lower = jnp.where(first, pltpu.roll(low, SLOTS, 1), high)
        ensemble = jnp.concatenate([upper, lower], axis=0).astype(BF16)
        part = dot(ensemble, one_hot(rows + chip * 2 * SLOTS == table_ref[SLOT : SLOT + 1]))
        total = part if total is None else total + part
    prior_ref[...] = total.astype(BF16)


def second_kernel(
    own_ref, beside_ref, errors_ref, table_ref, mean_ref, anom_ref, taper_ref,
    new_mean_ref, new_anom_ref, scaled_ref,
):
    members = anom_ref.shape[1]
    ensemble = jnp.concatenate([beside_ref[0], own_ref[...], beside_ref[1]], axis=1)
    listed = jnp.concatenate([ensemble, errors_ref[...]], axis=0)
    update_tiles(
        listed, table_ref, 1, members, members + 2, mean_ref, anom_ref, taper_ref,
        new_mean_ref, new_anom_ref, scaled_ref, None,
    )


def beside(rows, chips, states):
    at = lambda state, chip, core: (state * chips + chip) * 2 + core
    groups = [[at(s, c, 1), at(s + 1, c, 0)] for s in range(states - 1) for c in range(chips)]
    for state, core in ((0, 0), (states - 1, 1)):
        groups += [[at(state, c, core), at(state, c + 1, core)] for c in range(0, chips, 2)]
    swapped = lax.all_gather(rows, ("state", "chip", "core"), axis_index_groups=groups)
    partner = jnp.where(lax.axis_index("core") == 1, swapped[1], swapped[0])
    return lax.all_gather(partner, "core")


def across_two(own, pair, crowded, chips, states):
    at = lambda state, chip, core: (state * chips + chip) * 2 + core
    groups = [
        [at(s, c, 1) for c in range(chips)] + [at((s + 1) % states, c, 0) for c in range(chips)] for s in range(states)
    ]
    pair = lax.all_gather(pair, "core")
    low = (lax.iota(jnp.int32, 2 * chips) < chips) == (lax.axis_index("core") == 1)
    sent = jnp.where(low[:, None, None], own[None], (pair[0] + pair[1])[None])
    dealt = lax.all_to_all(sent, ("state", "chip", "core"), 0, 0, axis_index_groups=groups)
    return lax.optimization_barrier((lax.all_gather(dealt, "core"), crowded))


def local(state_mean, state_anom, obs_prior, obs_value, obs_var, obs_weight, obs_home, tile_obs, taper):
    tiles, members, cells = state_anom.shape
    tile_width = taper.shape[3]
    chips, states = lax.axis_size("chip"), lax.axis_size("state")
    width = obs_prior.shape[2]
    region = 2 * chips * width
    raw = (jnp.swapaxes(obs_prior, 1, 2), obs_value, obs_var, obs_home[None], tile_obs, state_mean)
    block = jax.ShapeDtypeStruct((width * 3 // 2, LANES), BF16)
    own, pair, table, mean, crowded = pl.pallas_call(
        functools.partial(prepare_kernel, chips, tile_width),
        out_shape=(
            block,
            block,
            jax.ShapeDtypeStruct((8, region), jnp.int32),
            jax.ShapeDtypeStruct(state_mean.shape, state_mean.dtype),
            pltpu.SMEM((1,), jnp.int32),
        ),
        in_specs=[pl.BlockSpec(memory_space=pltpu.HBM)] * len(raw),
        out_specs=(VMEM, VMEM, VMEM, VMEM, SMEM),
        scratch_shapes=[pltpu.VMEM(a.shape, a.dtype) for a in raw[:-1]] + [pltpu.SemaphoreType.DMA((len(raw),))],
        compiler_params=SMALL,
        name="prepare",
    )(*[pltpu.with_memory_space_constraint(a, pltpu.HBM) for a in raw])
    records, crowded = across_two(own, pair, crowded, chips, states)

    state_shapes = (
        jax.ShapeDtypeStruct(state_mean.shape, state_mean.dtype),
        jax.ShapeDtypeStruct(state_anom.shape, state_anom.dtype),
    )
    scaled = pltpu.VMEM((tiles, tile_obs.shape[2], cells), BF16)
    prior_shape = jax.ShapeDtypeStruct((members, region), BF16)
    new_mean, new_anom, packed, prior, errors = pl.pallas_call(
        first_kernel,
        out_shape=state_shapes
        + (
            jax.ShapeDtypeStruct((members // 2, LANES), BF16),
            prior_shape,
            jax.ShapeDtypeStruct((16, 3 * region), BF16),
        ),
        in_specs=[VMEM] * 6,
        out_specs=(VMEM,) * 5,
        scratch_shapes=[
            pltpu.VMEM((4 * region, LANES), BF16),
            scaled,
            pltpu.VMEM((cells // tile_width, 2 * members + 16, tiles * tile_width), BF16),
        ],
        compiler_params=LARGE,
        name="first",
    )(records, table, obs_weight, mean, state_anom, taper)

    def to_row(part):
        return lax.all_to_all(jnp.broadcast_to(part[None], (chips,) + part.shape), "chip", 0, 0)

    def by_slot(packed, prior, table):
        return pl.pallas_call(
            spread_kernel,
            out_shape=prior_shape,
            in_specs=[VMEM] * 2,
            out_specs=VMEM,
            compiler_params=SMALL,
            name="spread",
        )(lax.all_gather(to_row(packed), "core"), table)

    def whole(packed, prior, table):
        both = lax.all_gather(prior, "core")
        return jnp.sum(to_row(both[0] + both[1]), axis=0, dtype=BF16)

    prior_row = lax.cond(crowded[0] == 0, by_slot, whole, packed, prior, table)
    sides = beside(prior_row, chips, states)

    return pl.pallas_call(
        second_kernel,
        out_shape=state_shapes,
        in_specs=[VMEM] * 7,
        out_specs=(VMEM,) * 2,
        scratch_shapes=[scaled],
        compiler_params=LARGE,
        name="second",
    )(prior_row, sides, errors, table, new_mean, new_anom, taper)


def solution(mesh):
    states, columns = mesh.shape["state"], mesh.shape["obs"]
    fine = Mesh(mesh.devices.reshape(states, columns // 2, 2), ("state", "chip", "core"))
    every = ("state", "chip", "core")
    in_specs = (
        P(every, None),
        P(every, None, None),
        P(None, None, every),
        P(None, every),
        P(None, every),
        P(None, "state"),
        P("state"),
        P(None, every, None),
        P(None, every, None, None),
    )
    out_specs = (P(every, None), P(every, None, None))
    return jax.shard_map(local, mesh=fine, in_specs=in_specs, out_specs=out_specs, check_vma=False)
```

```python
import jax
import jax.numpy as jnp
from jax import lax
from jax.experimental import pallas as pl
from jax.experimental.pallas import tpu as pltpu
from jax.sharding import Mesh
from jax.sharding import PartitionSpec as P

F32 = jnp.float32
BF16 = jnp.bfloat16
LANES = 128
SLOTS = 64
KEPT = 84
SLOT, MINE, NEAR, LISTS = 0, 1, 2, 3
VMEM = pl.BlockSpec(memory_space=pltpu.VMEM)
SMEM = pl.BlockSpec(memory_space=pltpu.SMEM)
SMALL = pltpu.CompilerParams(vmem_limit_bytes=8 * 1024 * 1024)
LARGE = pltpu.CompilerParams(vmem_limit_bytes=24 * 1024 * 1024)


def dot(a, b, contract=((1,), (0,))):
    return lax.dot_general(a, b, (contract, ((), ())), preferred_element_type=F32)


def iota(shape, dim):
    return lax.broadcasted_iota(jnp.int32, shape, dim)


def one_hot(mask):
    return jnp.where(mask, 1.0, 0.0).astype(BF16)


def identity(size):
    return one_hot(iota((size, size), 0) == iota((size, size), 1))


def pick(fields, ids):
    slots = fields.shape[1]
    step = 512
    total = None
    for start in range(0, slots, step):
        chosen = one_hot(iota((step, ids.shape[1]), 0) + start == ids)
        part = dot(fields[:, start : start + step], chosen)
        total = part if total is None else total + part
    return total


def package(ensemble, value, var):
    members = ensemble.shape[0]
    centre = jnp.sum(ensemble, axis=0, keepdims=True) / members
    anomaly = ensemble - centre
    spread = jnp.sum(anomaly * anomaly, axis=0, keepdims=True) / (members - 1)
    gain = 1.0 / (spread + var)
    factor = 1.0 / (1.0 + jnp.sqrt(var * gain))
    coef_anom = factor * gain / (members - 1)
    coef_mean = gain * (value - centre) / (members - 1)
    return anomaly, coef_anom, coef_mean


def scale_tile(basis, coefs, mean_ref, anom_ref, taper, tile, new_mean_ref, scaled_ref):
    taper = taper.astype(F32)
    taper_anom = taper * coefs[:, 0:1]
    taper_mean = taper * coefs[:, 1:2]
    width = taper.shape[1]
    step = 2 * width
    for start in range(0, anom_ref.shape[2], step):
        projection = dot(basis, anom_ref[tile, :, start : start + step], ((0,), (0,)))
        for part in range(0, step, width):
            cells = slice(start + part, start + part + width)
            level = projection[:, part : part + width]
            scaled_ref[tile, :, cells] = (taper_anom * level).astype(BF16)
            shift = jnp.sum(taper_mean * level, axis=0, keepdims=True)
            new_mean_ref[tile : tile + 1, cells] = mean_ref[tile : tile + 1, cells] + shift


def shift_tile(basis, mean_ref, anom_ref, tile, new_mean_ref, new_anom_ref, scaled_ref, width, change_ref):
    step = 2 * width
    for start in range(0, anom_ref.shape[2], step):
        cells = slice(start, start + step)
        old = anom_ref[tile, :, cells].astype(F32)
        new_anom = (old - dot(basis, scaled_ref[tile, :, cells])).astype(BF16)
        new_anom_ref[tile, :, cells] = new_anom
        if change_ref is not None:
            rise = new_mean_ref[tile : tile + 1, cells] - mean_ref[tile : tile + 1, cells]
            high = rise.astype(BF16).astype(F32)
            middle = (rise - high).astype(BF16).astype(F32)
            row = iota((16, step), 0)
            rises = jnp.where(row == 0, high, jnp.where(row == 1, middle, jnp.where(row == 2, rise - high - middle, 0.0)))
            stack = (new_anom, anom_ref[tile, :, cells], rises.astype(BF16))
            for part in range(2):
                at = 0
                for values in stack:
                    change_ref[start // width + part, at : at + values.shape[0], tile * width : (tile + 1) * width] = values[
                        :, part * width : (part + 1) * width
                    ]
                    at += values.shape[0]


def update_tiles(
    listed, table_ref, colour, members, value_row, mean_ref, anom_ref, taper_ref,
    new_mean_ref, new_anom_ref, scaled_ref, change_ref,
):
    tiles, length = taper_ref.shape[1], taper_ref.shape[2]
    picked = pick(listed, table_ref[LISTS + colour : LISTS + colour + 1])
    anomaly, coef_anom, coef_mean = package(
        picked[:members], picked[value_row : value_row + 1], picked[value_row + 1 : value_row + 2]
    )
    basis = anomaly.astype(BF16)
    coefs = jnp.concatenate([coef_anom, coef_mean, jnp.zeros((6, tiles * length), F32)], axis=0).T
    for tile in range(tiles):
        own = slice(tile * length, (tile + 1) * length)
        scale_tile(
            basis[:, own], coefs[own], mean_ref, anom_ref, taper_ref[colour, tile], tile, new_mean_ref, scaled_ref
        )
    for tile in range(tiles):
        own = slice(tile * length, (tile + 1) * length)
        shift_tile(
            basis[:, own], mean_ref, anom_ref, tile, new_mean_ref, new_anom_ref, scaled_ref, taper_ref.shape[3],
            change_ref,
        )


def fold(block, other):
    other = pltpu.roll(other, KEPT, 1)
    lane = iota(block.shape, 1)
    half = block.shape[0] // 2
    beneath = jnp.where(lane[:half] < LANES // 2, other[:half], pltpu.roll(other[half:], LANES // 2, 1))
    return jnp.concatenate([jnp.where(lane < KEPT, block, other), beneath], axis=0).astype(BF16)


def unfold(folded):
    folded = folded.astype(F32)
    width = folded.shape[0] * 2 // 3
    beneath = folded[width:]
    other = jnp.concatenate([beneath, pltpu.roll(beneath, LANES // 2, 1)], axis=0)
    return jnp.where(iota((width, LANES), 1) < KEPT, other, folded[:width]).astype(BF16)


def prepare_kernel(
    prior_in, value_in, var_in, home_in, lists_in, mean_in,
    own_ref, pair_ref, home_ref, lists_ref, mean_ref, prior_ref, value_ref, var_ref, sems,
):
    copies = [
        pltpu.make_async_copy(source, target, sems.at[i])
        for i, (source, target) in enumerate(
            (
                (prior_in, prior_ref), (value_in, value_ref), (var_in, var_ref), (home_in, home_ref), (lists_in, lists_ref),
                (mean_in, mean_ref),
            )
        )
    ]
    for copy in copies:
        copy.start()
    for copy in copies:
        copy.wait()
    _, width, members = prior_ref.shape
    row = iota((LANES, width), 0) - members
    value = value_ref[...].astype(F32)
    var = var_ref[...].astype(F32)
    tail = jnp.where(row == 0, value[0:1], 0.0)
    tail = jnp.where(row == 1, var[0:1], tail)
    tail = jnp.where(row == 2, value[1:2], tail)
    tail = jnp.where(row == 3, var[1:2], tail).astype(BF16)
    widen = one_hot(iota((members, LANES), 0) == iota((members, LANES), 1))
    first = dot(prior_ref[0], widen) + dot(identity(width), tail, ((1,), (1,)))
    second = dot(prior_ref[1], widen)
    none = jnp.zeros_like(first)
    on_first = lax.axis_index("core") == 0
    own_ref[...] = fold(first, second)
    pair_ref[...] = fold(jnp.where(on_first, first, none), jnp.where(on_first, none, first))


def plan(chips, tile_columns, home_ref, lists_ref, table_ref, crowded_ref):
    colours, tiles, length = lists_ref.shape
    region = home_ref.shape[1]
    state, own_chip, core = lax.axis_index("state"), lax.axis_index("chip"), lax.axis_index("core")
    device_columns = tiles * tile_columns
    own = own_chip * 2 + core
    column = home_ref[...] - state * (chips * 2 * device_columns)
    first_column = iota((2 * chips, region), 0) * device_columns
    at_home = (column >= first_column) & (column < first_column + device_columns)
    at_home = jnp.where(at_home, 1.0, 0.0)
    earlier = one_hot(iota((LANES, LANES), 0) < iota((LANES, LANES), 1))
    ranks, before = [], jnp.zeros((2 * chips, 1), F32)
    for start in range(0, region, LANES):
        some = at_home[:, start : start + LANES]
        ranks.append(jnp.sum(some * (dot(some.astype(BF16), earlier) + before), axis=0, keepdims=True))
        before = before + jnp.sum(some, axis=1, keepdims=True)
    rank = jnp.concatenate(ranks, axis=1)
    device = jnp.sum(at_home * iota((2 * chips, region), 0).astype(F32), axis=0, keepdims=True)
    slot = (device * SLOTS + rank).astype(jnp.int32)
    table_ref[SLOT : SLOT + 1] = slot
    table_ref[MINE : MINE + 1] = slot - own * SLOTS
    table_ref[NEAR : NEAR + 1] = column - own * device_columns
    for colour in range(colours):
        for tile in range(tiles):
            table_ref[LISTS + colour : LISTS + colour + 1, tile * length : (tile + 1) * length] = (
                lists_ref[colour, tile : tile + 1] - (state - 1) * region
            )
    crowded_ref[0] = (jnp.max(rank) >= SLOTS).astype(jnp.int32)


def first_kernel(
    records_ref, home_ref, lists_ref, weight_ref, mean_ref, anom_ref, taper_ref,
    new_mean_ref, new_anom_ref, packed_ref, prior_ref, errors_ref, table_ref, crowded_ref, rows_ref, scaled_ref, change_ref,
):
    members = anom_ref.shape[1]
    _, dealt, height, _ = records_ref.shape
    chips, width = dealt // 2, height * 2 // 3
    region = 2 * chips * width
    plan(chips, taper_ref.shape[3], home_ref, lists_ref, table_ref, crowded_ref)
    for chip in range(chips):
        at = chip * 2 * width
        for side, part in ((0, 0), (1, 2)):
            folded = records_ref[side, side * chips + chip]
            rows_ref[part * region + at : part * region + at + width] = folded[:width]
            rows_ref[part * region + at + width : part * region + at + 2 * width] = unfold(folded)
        for core in range(2):
            folded = records_ref[core, chip + (1 - core) * chips]
            here = at + core * width
            rows_ref[region + here : region + here + width] = folded[:width]
            rows_ref[3 * region + here : 3 * region + here + width] = unfold(folded)
    count = members + 16
    field, lane = iota((count, LANES), 0), iota((count, LANES), 1)
    plain = one_hot(field == lane)
    turned = one_hot(jnp.where(field < LANES - KEPT, field + KEPT, field + KEPT - LANES) == lane)
    both = jnp.concatenate([plain, turned], axis=0)
    on_first = jnp.bitwise_and(iota((count, region), 1), 2 * width - 1) < width
    listed = []
    for part in range(3):
        rows = rows_ref[part * region : (part + 1) * region]
        if part == 1:
            listed.append(dot(plain, rows, ((1,), (1,))).astype(BF16))
        else:
            fields = dot(both, rows, ((1,), (1,)))
            listed.append(jnp.where(on_first, fields[:count], fields[count:]).astype(BF16))
    listed = jnp.concatenate(listed, axis=1)
    prior = dot(turned[:members], rows_ref[3 * region :], ((1,), (1,)))
    errors_ref[...] = listed[members:]
    update_tiles(
        listed, table_ref, 0, members, members, mean_ref, anom_ref, taper_ref,
        new_mean_ref, new_anom_ref, scaled_ref, change_ref,
    )
    home = table_ref[NEAR : NEAR + 1]
    columns = change_ref.shape[2]
    at_home = one_hot(iota((columns, region), 0) == home)
    increment = None
    for level in range(change_ref.shape[0]):
        chosen = dot(change_ref[level], at_home)
        rise = chosen[2 * members : 2 * members + 1] + chosen[2 * members + 1 : 2 * members + 2]
        rise = rise + chosen[2 * members + 2 : 2 * members + 3]
        part = (chosen[:members] - chosen[members : 2 * members] + rise) * weight_ref[level : level + 1]
        increment = part if increment is None else increment + part
    inside = (home >= 0) & (home < columns)
    updated = jnp.where(inside, prior + increment, 0.0).astype(BF16)
    prior_ref[...] = updated
    lane = iota((LANES, region), 0)
    to_slot = one_hot(jnp.where(lane < SLOTS, lane, lane - SLOTS) == table_ref[MINE : MINE + 1])
    twice = dot(updated, to_slot, ((1,), (1,)))
    half = members // 2
    packed_ref[...] = jnp.where(iota((half, LANES), 1) < SLOTS, twice[:half], twice[half:]).astype(BF16)


def spread_kernel(packed_ref, table_ref, prior_ref):
    region = table_ref.shape[1]
    _, chips, half, _ = packed_ref.shape
    first = iota((half, LANES), 1) < SLOTS
    rows = iota((2 * SLOTS, region), 0)
    total = None
    for chip in range(chips):
        low, high = packed_ref[0, chip].astype(F32), packed_ref[1, chip].astype(F32)
        upper = jnp.where(first, low, pltpu.roll(high, SLOTS, 1))
        lower = jnp.where(first, pltpu.roll(low, SLOTS, 1), high)
        ensemble = jnp.concatenate([upper, lower], axis=0).astype(BF16)
        part = dot(ensemble, one_hot(rows + chip * 2 * SLOTS == table_ref[SLOT : SLOT + 1]))
        total = part if total is None else total + part
    prior_ref[...] = total.astype(BF16)


def second_kernel(
    own_ref, beside_ref, errors_ref, table_ref, mean_ref, anom_ref, taper_ref,
    new_mean_ref, new_anom_ref, scaled_ref,
):
    members = anom_ref.shape[1]
    ensemble = jnp.concatenate([beside_ref[0], own_ref[...], beside_ref[1]], axis=1)
    listed = jnp.concatenate([ensemble, errors_ref[...]], axis=0)
    update_tiles(
        listed, table_ref, 1, members, members + 2, mean_ref, anom_ref, taper_ref,
        new_mean_ref, new_anom_ref, scaled_ref, None,
    )


def beside(rows, chips, states):
    at = lambda state, chip, core: (state * chips + chip) * 2 + core
    groups = [[at(s, c, 1), at(s + 1, c, 0)] for s in range(states - 1) for c in range(chips)]
    for state, core in ((0, 0), (states - 1, 1)):
        groups += [[at(state, c, core), at(state, c + 1, core)] for c in range(0, chips, 2)]
    swapped = lax.all_gather(rows, ("state", "chip", "core"), axis_index_groups=groups)
    partner = jnp.where(lax.axis_index("core") == 1, swapped[1], swapped[0])
    return lax.all_gather(partner, "core")


def across_two(own, pair, chips, states):
    at = lambda state, chip, core: (state * chips + chip) * 2 + core
    groups = [
        [at(s, c, 1) for c in range(chips)] + [at((s + 1) % states, c, 0) for c in range(chips)] for s in range(states)
    ]
    pair = lax.all_gather(pair, "core")
    low = (lax.iota(jnp.int32, 2 * chips) < chips) == (lax.axis_index("core") == 1)
    sent = jnp.where(low[:, None, None], own[None], (pair[0] + pair[1])[None])
    dealt = lax.all_to_all(sent, ("state", "chip", "core"), 0, 0, axis_index_groups=groups)
    return lax.all_gather(dealt, "core")


def local(state_mean, state_anom, obs_prior, obs_value, obs_var, obs_weight, obs_home, tile_obs, taper):
    tiles, members, cells = state_anom.shape
    tile_width = taper.shape[3]
    chips, states = lax.axis_size("chip"), lax.axis_size("state")
    width = obs_prior.shape[2]
    region = 2 * chips * width
    raw = (jnp.swapaxes(obs_prior, 1, 2), obs_value, obs_var, obs_home[None], tile_obs, state_mean)
    block = jax.ShapeDtypeStruct((width * 3 // 2, LANES), BF16)
    own, pair, home, lists, mean = pl.pallas_call(
        prepare_kernel,
        out_shape=(
            block,
            block,
            *(jax.ShapeDtypeStruct(a.shape, a.dtype) for a in raw[3:]),
        ),
        in_specs=[pl.BlockSpec(memory_space=pltpu.HBM)] * len(raw),
        out_specs=(VMEM,) * 5,
        scratch_shapes=[pltpu.VMEM(a.shape, a.dtype) for a in raw[:3]] + [pltpu.SemaphoreType.DMA((len(raw),))],
        compiler_params=SMALL,
        name="prepare",
    )(*[pltpu.with_memory_space_constraint(a, pltpu.HBM) for a in raw])
    records = across_two(own, pair, chips, states)

    state_shapes = (
        jax.ShapeDtypeStruct(state_mean.shape, state_mean.dtype),
        jax.ShapeDtypeStruct(state_anom.shape, state_anom.dtype),
    )
    scaled = pltpu.VMEM((tiles, tile_obs.shape[2], cells), BF16)
    prior_shape = jax.ShapeDtypeStruct((members, region), BF16)
    new_mean, new_anom, packed, prior, errors, table, crowded = pl.pallas_call(
        first_kernel,
        out_shape=state_shapes
        + (
            jax.ShapeDtypeStruct((members // 2, LANES), BF16),
            prior_shape,
            jax.ShapeDtypeStruct((16, 3 * region), BF16),
            jax.ShapeDtypeStruct((8, region), jnp.int32),
            pltpu.SMEM((1,), jnp.int32),
        ),
        in_specs=[VMEM] * 7,
        out_specs=(VMEM,) * 6 + (SMEM,),
        scratch_shapes=[
            pltpu.VMEM((4 * region, LANES), BF16),
            scaled,
            pltpu.VMEM((cells // tile_width, 2 * members + 16, tiles * tile_width), BF16),
        ],
        compiler_params=LARGE,
        name="first",
    )(records, home, lists, obs_weight, mean, state_anom, taper)

    def to_row(part):
        return lax.all_to_all(jnp.broadcast_to(part[None], (chips,) + part.shape), "chip", 0, 0)

    def by_slot(packed, prior, table):
        return pl.pallas_call(
            spread_kernel,
            out_shape=prior_shape,
            in_specs=[VMEM] * 2,
            out_specs=VMEM,
            compiler_params=SMALL,
            name="spread",
        )(lax.all_gather(to_row(packed), "core"), table)

    def whole(packed, prior, table):
        both = lax.all_gather(prior, "core")
        return jnp.sum(to_row(both[0] + both[1]), axis=0, dtype=BF16)

    prior_row = lax.cond(crowded[0] == 0, by_slot, whole, packed, prior, table)
    sides = beside(prior_row, chips, states)

    return pl.pallas_call(
        second_kernel,
        out_shape=state_shapes,
        in_specs=[VMEM] * 7,
        out_specs=(VMEM,) * 2,
        scratch_shapes=[scaled],
        compiler_params=LARGE,
        name="second",
    )(prior_row, sides, errors, table, new_mean, new_anom, taper)


def solution(mesh):
    states, columns = mesh.shape["state"], mesh.shape["obs"]
    fine = Mesh(mesh.devices.reshape(states, columns // 2, 2), ("state", "chip", "core"))
    every = ("state", "chip", "core")
    in_specs = (
        P(every, None),
        P(every, None, None),
        P(None, None, every),
        P(None, every),
        P(None, every),
        P(None, "state"),
        P("state"),
        P(None, every, None),
        P(None, every, None, None),
    )
    out_specs = (P(every, None), P(every, None, None))
    return jax.shard_map(local, mesh=fine, in_specs=in_specs, out_specs=out_specs, check_vma=False)
```

```python
import functools

import jax
import jax.numpy as jnp
from jax import lax
from jax.experimental import pallas as pl
from jax.experimental.pallas import tpu as pltpu
from jax.sharding import Mesh
from jax.sharding import PartitionSpec as P

F32 = jnp.float32
BF16 = jnp.bfloat16
LANES = 128
SLOTS = 64
KEPT = 84
SLOT, MINE, NEAR, LISTS = 0, 1, 2, 3
VMEM = pl.BlockSpec(memory_space=pltpu.VMEM)
SMEM = pl.BlockSpec(memory_space=pltpu.SMEM)
SMALL = pltpu.CompilerParams(vmem_limit_bytes=8 * 1024 * 1024)
LARGE = pltpu.CompilerParams(vmem_limit_bytes=24 * 1024 * 1024)


def dot(a, b, contract=((1,), (0,))):
    return lax.dot_general(a, b, (contract, ((), ())), preferred_element_type=F32)


def iota(shape, dim):
    return lax.broadcasted_iota(jnp.int32, shape, dim)


def one_hot(mask):
    return jnp.where(mask, 1.0, 0.0).astype(BF16)


def identity(size):
    return one_hot(iota((size, size), 0) == iota((size, size), 1))


def pick(fields, ids):
    slots = fields.shape[1]
    step = 512
    total = None
    for start in range(0, slots, step):
        chosen = one_hot(iota((step, ids.shape[1]), 0) + start == ids)
        part = dot(fields[:, start : start + step], chosen)
        total = part if total is None else total + part
    return total


def package(ensemble, value, var):
    members = ensemble.shape[0]
    centre = jnp.sum(ensemble, axis=0, keepdims=True) / members
    anomaly = ensemble - centre
    spread = jnp.sum(anomaly * anomaly, axis=0, keepdims=True) / (members - 1)
    gain = 1.0 / (spread + var)
    factor = 1.0 / (1.0 + jnp.sqrt(var * gain))
    coef_anom = factor * gain / (members - 1)
    coef_mean = gain * (value - centre) / (members - 1)
    return anomaly, coef_anom, coef_mean


def scale_tile(basis, coefs, mean_ref, anom_ref, taper, tile, new_mean_ref, scaled_ref):
    taper = taper.astype(F32)
    taper_anom = taper * coefs[:, 0:1]
    taper_mean = taper * coefs[:, 1:2]
    width = taper.shape[1]
    step = 2 * width
    for start in range(0, anom_ref.shape[2], step):
        projection = dot(basis, anom_ref[tile, :, start : start + step], ((0,), (0,)))
        for part in range(0, step, width):
            cells = slice(start + part, start + part + width)
            level = projection[:, part : part + width]
            scaled_ref[tile, :, cells] = (taper_anom * level).astype(BF16)
            shift = jnp.sum(taper_mean * level, axis=0, keepdims=True)
            new_mean_ref[tile : tile + 1, cells] = mean_ref[tile : tile + 1, cells] + shift


def shift_tile(basis, mean_ref, anom_ref, tile, new_mean_ref, new_anom_ref, scaled_ref, width, change_ref):
    step = 2 * width
    for start in range(0, anom_ref.shape[2], step):
        cells = slice(start, start + step)
        old = anom_ref[tile, :, cells].astype(F32)
        new_anom = (old - dot(basis, scaled_ref[tile, :, cells])).astype(BF16)
        new_anom_ref[tile, :, cells] = new_anom
        if change_ref is not None:
            rise = new_mean_ref[tile : tile + 1, cells] - mean_ref[tile : tile + 1, cells]
            high = rise.astype(BF16).astype(F32)
            middle = (rise - high).astype(BF16).astype(F32)
            row = iota((16, step), 0)
            rises = jnp.where(row == 0, high, jnp.where(row == 1, middle, jnp.where(row == 2, rise - high - middle, 0.0)))
            stack = (new_anom, anom_ref[tile, :, cells], rises.astype(BF16))
            for part in range(2):
                at = 0
                for values in stack:
                    change_ref[start // width + part, at : at + values.shape[0], tile * width : (tile + 1) * width] = values[
                        :, part * width : (part + 1) * width
                    ]
                    at += values.shape[0]


def update_tiles(
    listed, table_ref, colour, members, value_row, mean_ref, anom_ref, taper_ref,
    new_mean_ref, new_anom_ref, scaled_ref, change_ref,
):
    tiles, length = taper_ref.shape[1], taper_ref.shape[2]
    picked = pick(listed, table_ref[LISTS + colour : LISTS + colour + 1])
    anomaly, coef_anom, coef_mean = package(
        picked[:members], picked[value_row : value_row + 1], picked[value_row + 1 : value_row + 2]
    )
    basis = anomaly.astype(BF16)
    coefs = jnp.concatenate([coef_anom, coef_mean, jnp.zeros((6, tiles * length), F32)], axis=0).T
    for tile in range(tiles):
        own = slice(tile * length, (tile + 1) * length)
        scale_tile(
            basis[:, own], coefs[own], mean_ref, anom_ref, taper_ref[colour, tile], tile, new_mean_ref, scaled_ref
        )
    for tile in range(tiles):
        own = slice(tile * length, (tile + 1) * length)
        shift_tile(
            basis[:, own], mean_ref, anom_ref, tile, new_mean_ref, new_anom_ref, scaled_ref, taper_ref.shape[3],
            change_ref,
        )


def fold(block, other):
    other = pltpu.roll(other, KEPT, 1)
    lane = iota(block.shape, 1)
    half = block.shape[0] // 2
    beneath = jnp.where(lane[:half] < LANES // 2, other[:half], pltpu.roll(other[half:], LANES // 2, 1))
    return jnp.concatenate([jnp.where(lane < KEPT, block, other), beneath], axis=0).astype(BF16)


def unfold(folded):
    folded = folded.astype(F32)
    width = folded.shape[0] * 2 // 3
    beneath = folded[width:]
    other = jnp.concatenate([beneath, pltpu.roll(beneath, LANES // 2, 1)], axis=0)
    return jnp.where(iota((width, LANES), 1) < KEPT, other, folded[:width]).astype(BF16)


def prepare_kernel(
    chips, tile_columns, prior_in, value_in, var_in, home_in, lists_in, mean_in,
    own_ref, pair_ref, table_ref, mean_ref, crowded_ref, prior_ref, value_ref, var_ref, home_ref, lists_ref, sems,
):
    copies = [
        pltpu.make_async_copy(source, target, sems.at[i])
        for i, (source, target) in enumerate(
            (
                (prior_in, prior_ref), (value_in, value_ref), (var_in, var_ref), (home_in, home_ref), (lists_in, lists_ref),
                (mean_in, mean_ref),
            )
        )
    ]
    for copy in copies:
        copy.start()
    for copy in copies:
        copy.wait()
    _, width, members = prior_ref.shape
    row = iota((LANES, width), 0) - members
    value = value_ref[...].astype(F32)
    var = var_ref[...].astype(F32)
    tail = jnp.where(row == 0, value[0:1], 0.0)
    tail = jnp.where(row == 1, var[0:1], tail)
    tail = jnp.where(row == 2, value[1:2], tail)
    tail = jnp.where(row == 3, var[1:2], tail).astype(BF16)
    widen = one_hot(iota((members, LANES), 0) == iota((members, LANES), 1))
    first = dot(prior_ref[0], widen) + dot(identity(width), tail, ((1,), (1,)))
    second = dot(prior_ref[1], widen)
    none = jnp.zeros_like(first)
    on_first = lax.axis_index("core") == 0
    own_ref[...] = fold(first, second)
    pair_ref[...] = fold(jnp.where(on_first, first, none), jnp.where(on_first, none, first))
    colours, tiles, length = lists_ref.shape
    region = home_ref.shape[1]
    state, own_chip, core = lax.axis_index("state"), lax.axis_index("chip"), lax.axis_index("core")
    device_columns = tiles * tile_columns
    own = own_chip * 2 + core
    column = home_ref[...] - state * (chips * 2 * device_columns)
    first_column = iota((2 * chips, region), 0) * device_columns
    at_home = (column >= first_column) & (column < first_column + device_columns)
    at_home = jnp.where(at_home, 1.0, 0.0)
    earlier = one_hot(iota((LANES, LANES), 0) < iota((LANES, LANES), 1))
    ranks, before = [], jnp.zeros((2 * chips, 1), F32)
    for start in range(0, region, LANES):
        some = at_home[:, start : start + LANES]
        ranks.append(jnp.sum(some * (dot(some.astype(BF16), earlier) + before), axis=0, keepdims=True))
        before = before + jnp.sum(some, axis=1, keepdims=True)
    rank = jnp.concatenate(ranks, axis=1)
    device = jnp.sum(at_home * iota((2 * chips, region), 0).astype(F32), axis=0, keepdims=True)
    slot = (device * SLOTS + rank).astype(jnp.int32)
    table_ref[SLOT : SLOT + 1] = slot
    table_ref[MINE : MINE + 1] = slot - own * SLOTS
    table_ref[NEAR : NEAR + 1] = column - own * device_columns
    for colour in range(colours):
        for tile in range(tiles):
            table_ref[LISTS + colour : LISTS + colour + 1, tile * length : (tile + 1) * length] = (
                lists_ref[colour, tile : tile + 1] - (state - 1) * region
            )
    crowded_ref[0] = (jnp.max(rank) >= SLOTS).astype(jnp.int32)


def first_kernel(
    records_ref, table_ref, weight_ref, mean_ref, anom_ref, taper_ref,
    new_mean_ref, new_anom_ref, packed_ref, prior_ref, errors_ref, rows_ref, scaled_ref, change_ref,
):
    members = anom_ref.shape[1]
    _, dealt, folded_rows, _ = records_ref.shape
    chips, width = dealt // 2, folded_rows * 2 // 3
    region = 2 * chips * width
    for chip in range(chips):
        at = chip * 2 * width
        for side, part in ((0, 0), (1, 2)):
            folded = records_ref[side, side * chips + chip]
            rows_ref[part * region + at : part * region + at + width] = folded[:width]
            rows_ref[part * region + at + width : part * region + at + 2 * width] = unfold(folded)
        for core in range(2):
            folded = records_ref[core, chip + (1 - core) * chips]
            here = at + core * width
            rows_ref[region + here : region + here + width] = folded[:width]
            rows_ref[3 * region + here : 3 * region + here + width] = unfold(folded)
    count = members + 16
    field, lane = iota((count, LANES), 0), iota((count, LANES), 1)
    plain = one_hot(field == lane)
    turned = one_hot(jnp.where(field < LANES - KEPT, field + KEPT, field + KEPT - LANES) == lane)
    both = jnp.concatenate([plain, turned], axis=0)
    on_first = jnp.bitwise_and(iota((count, region), 1), 2 * width - 1) < width
    listed = []
    for part in range(3):
        rows = rows_ref[part * region : (part + 1) * region]
        if part == 1:
            listed.append(dot(plain, rows, ((1,), (1,))).astype(BF16))
        else:
            fields = dot(both, rows, ((1,), (1,)))
            listed.append(jnp.where(on_first, fields[:count], fields[count:]).astype(BF16))
    listed = jnp.concatenate(listed, axis=1)
    prior = dot(turned[:members], rows_ref[3 * region :], ((1,), (1,)))
    errors_ref[...] = listed[members:]
    update_tiles(
        listed, table_ref, 0, members, members, mean_ref, anom_ref, taper_ref,
        new_mean_ref, new_anom_ref, scaled_ref, change_ref,
    )
    home = table_ref[NEAR : NEAR + 1]
    columns = change_ref.shape[2]
    at_home = one_hot(iota((columns, region), 0) == home)
    increment = None
    levels, height, _ = change_ref.shape
    together = 4
    for start in range(0, levels, together):
        several = change_ref[start : start + together].reshape(together * height, columns)
        several = dot(several, at_home)
        for level in range(start, start + together):
            chosen = several[(level - start) * height : (level - start + 1) * height]
            rise = chosen[2 * members : 2 * members + 1] + chosen[2 * members + 1 : 2 * members + 2]
            rise = rise + chosen[2 * members + 2 : 2 * members + 3]
            part = (chosen[:members] - chosen[members : 2 * members] + rise) * weight_ref[level : level + 1]
            increment = part if increment is None else increment + part
    inside = (home >= 0) & (home < columns)
    updated = jnp.where(inside, prior + increment, 0.0).astype(BF16)
    prior_ref[...] = updated
    lane = iota((LANES, region), 0)
    to_slot = one_hot(jnp.where(lane < SLOTS, lane, lane - SLOTS) == table_ref[MINE : MINE + 1])
    twice = dot(updated, to_slot, ((1,), (1,)))
    half = members // 2
    packed_ref[...] = jnp.where(iota((half, LANES), 1) < SLOTS, twice[:half], twice[half:]).astype(BF16)


def spread_kernel(packed_ref, table_ref, prior_ref):
    region = table_ref.shape[1]
    _, chips, half, _ = packed_ref.shape
    first = iota((half, LANES), 1) < SLOTS
    rows = iota((2 * SLOTS, region), 0)
    total = None
    for chip in range(chips):
        low, high = packed_ref[0, chip].astype(F32), packed_ref[1, chip].astype(F32)
        upper = jnp.where(first, low, pltpu.roll(high, SLOTS, 1))
        lower = jnp.where(first, pltpu.roll(low, SLOTS, 1), high)
        ensemble = jnp.concatenate([upper, lower], axis=0).astype(BF16)
        part = dot(ensemble, one_hot(rows + chip * 2 * SLOTS == table_ref[SLOT : SLOT + 1]))
        total = part if total is None else total + part
    prior_ref[...] = total.astype(BF16)


def second_kernel(
    own_ref, beside_ref, errors_ref, table_ref, mean_ref, anom_ref, taper_ref,
    new_mean_ref, new_anom_ref, scaled_ref,
):
    members = anom_ref.shape[1]
    ensemble = jnp.concatenate([beside_ref[0], own_ref[...], beside_ref[1]], axis=1)
    listed = jnp.concatenate([ensemble, errors_ref[...]], axis=0)
    update_tiles(
        listed, table_ref, 1, members, members + 2, mean_ref, anom_ref, taper_ref,
        new_mean_ref, new_anom_ref, scaled_ref, None,
    )


def beside(rows, chips, states):
    at = lambda state, chip, core: (state * chips + chip) * 2 + core
    groups = [[at(s, c, 1), at(s + 1, c, 0)] for s in range(states - 1) for c in range(chips)]
    for state, core in ((0, 0), (states - 1, 1)):
        groups += [[at(state, c, core), at(state, c + 1, core)] for c in range(0, chips, 2)]
    swapped = lax.all_gather(rows, ("state", "chip", "core"), axis_index_groups=groups)
    partner = jnp.where(lax.axis_index("core") == 1, swapped[1], swapped[0])
    return lax.all_gather(partner, "core")


def across_two(own, pair, crowded, chips, states):
    at = lambda state, chip, core: (state * chips + chip) * 2 + core
    groups = [
        [at(s, c, 1) for c in range(chips)] + [at((s + 1) % states, c, 0) for c in range(chips)] for s in range(states)
    ]
    pair = lax.all_gather(pair, "core")
    low = (lax.iota(jnp.int32, 2 * chips) < chips) == (lax.axis_index("core") == 1)
    sent = jnp.where(low[:, None, None], own[None], (pair[0] + pair[1])[None])
    dealt = lax.all_to_all(sent, ("state", "chip", "core"), 0, 0, axis_index_groups=groups)
    return lax.optimization_barrier((lax.all_gather(dealt, "core"), crowded))


def local(state_mean, state_anom, obs_prior, obs_value, obs_var, obs_weight, obs_home, tile_obs, taper):
    tiles, members, cells = state_anom.shape
    tile_width = taper.shape[3]
    chips, states = lax.axis_size("chip"), lax.axis_size("state")
    width = obs_prior.shape[2]
    region = 2 * chips * width
    raw = (jnp.swapaxes(obs_prior, 1, 2), obs_value, obs_var, obs_home[None], tile_obs, state_mean)
    block = jax.ShapeDtypeStruct((width * 3 // 2, LANES), BF16)
    own, pair, table, mean, crowded = pl.pallas_call(
        functools.partial(prepare_kernel, chips, tile_width),
        out_shape=(
            block,
            block,
            jax.ShapeDtypeStruct((8, region), jnp.int32),
            jax.ShapeDtypeStruct(state_mean.shape, state_mean.dtype),
            pltpu.SMEM((1,), jnp.int32),
        ),
        in_specs=[pl.BlockSpec(memory_space=pltpu.HBM)] * len(raw),
        out_specs=(VMEM, VMEM, VMEM, VMEM, SMEM),
        scratch_shapes=[pltpu.VMEM(a.shape, a.dtype) for a in raw[:-1]] + [pltpu.SemaphoreType.DMA((len(raw),))],
        compiler_params=SMALL,
        name="prepare",
    )(*[pltpu.with_memory_space_constraint(a, pltpu.HBM) for a in raw])
    records, crowded = across_two(own, pair, crowded, chips, states)

    state_shapes = (
        jax.ShapeDtypeStruct(state_mean.shape, state_mean.dtype),
        jax.ShapeDtypeStruct(state_anom.shape, state_anom.dtype),
    )
    scaled = pltpu.VMEM((tiles, tile_obs.shape[2], cells), BF16)
    prior_shape = jax.ShapeDtypeStruct((members, region), BF16)
    new_mean, new_anom, packed, prior, errors = pl.pallas_call(
        first_kernel,
        out_shape=state_shapes
        + (
            jax.ShapeDtypeStruct((members // 2, LANES), BF16),
            prior_shape,
            jax.ShapeDtypeStruct((16, 3 * region), BF16),
        ),
        in_specs=[VMEM] * 6,
        out_specs=(VMEM,) * 5,
        scratch_shapes=[
            pltpu.VMEM((4 * region, LANES), BF16),
            scaled,
            pltpu.VMEM((cells // tile_width, 2 * members + 16, tiles * tile_width), BF16),
        ],
        compiler_params=LARGE,
        name="first",
    )(records, table, obs_weight, mean, state_anom, taper)

    def to_row(part):
        return lax.all_to_all(jnp.broadcast_to(part[None], (chips,) + part.shape), "chip", 0, 0)

    def by_slot(packed, prior, table):
        return pl.pallas_call(
            spread_kernel,
            out_shape=prior_shape,
            in_specs=[VMEM] * 2,
            out_specs=VMEM,
            compiler_params=SMALL,
            name="spread",
        )(lax.all_gather(to_row(packed), "core"), table)

    def whole(packed, prior, table):
        both = lax.all_gather(prior, "core")
        return jnp.sum(to_row(both[0] + both[1]), axis=0, dtype=BF16)

    prior_row = lax.cond(crowded[0] == 0, by_slot, whole, packed, prior, table)
    sides = beside(prior_row, chips, states)

    return pl.pallas_call(
        second_kernel,
        out_shape=state_shapes,
        in_specs=[VMEM] * 7,
        out_specs=(VMEM,) * 2,
        scratch_shapes=[scaled],
        compiler_params=LARGE,
        name="second",
    )(prior_row, sides, errors, table, new_mean, new_anom, taper)


def solution(mesh):
    states, columns = mesh.shape["state"], mesh.shape["obs"]
    fine = Mesh(mesh.devices.reshape(states, columns // 2, 2), ("state", "chip", "core"))
    every = ("state", "chip", "core")
    in_specs = (
        P(every, None),
        P(every, None, None),
        P(None, None, every),
        P(None, every),
        P(None, every),
        P(None, "state"),
        P("state"),
        P(None, every, None),
        P(None, every, None, None),
    )
    out_specs = (P(every, None), P(every, None, None))
    return jax.shard_map(local, mesh=fine, in_specs=in_specs, out_specs=out_specs, check_vma=False)
```
